128 devices in a mesh: ctx: 16 (over y, z), head: 8 (over x, core).
Axes of the slice: x: 4, y: 4, z: 4, core: 2. Of those that a mesh axis runs over, the one named last changes fastest.
Arguments:
- queries: bfloat16 [12288, 4096], P(('ctx', 'head')), may hold values from -64 to 64
- keys: bfloat16 [12288, 1024], P(('ctx', 'head')), may hold values from -6 to 6
- values: bfloat16 [12288, 1024], P(('ctx', 'head')), may hold values from -6 to 6
- grad_out: bfloat16 [12288, 4096], P(('ctx', 'head')), may hold values from -6 to 6
- parent: int32 [48], replicated, may hold values from -1 to 46, as said below
- subtree_end: int32 [12288], P('ctx'), may hold values from 0 to 255, as said below
Outputs:
- attn_out: bfloat16 [12288, 4096], P(('ctx', 'head'))
- grad_q: bfloat16 [12288, 4096], P(('ctx', 'head'))
- grad_k: bfloat16 [12288, 1024], P(('ctx', 'head'))
- grad_v: bfloat16 [12288, 1024], P(('ctx', 'head'))
The draws below stay inside these ranges and needn't reach their ends.
Inputs may be any that keep to these rules, and one draw needn't show every extreme that they name: Device c of ctx holds blocks c * 3 to (c + 1) * 3 - 1. Block 0 is the only root. A block that is not first on its device has its parent among the earlier blocks of its device, and the last block of each device has the block just before it as parent; the first block of device c > 0 has as parent the first block of an earlier device. Along parents, a block meets the first blocks of at most 4 other devices, and some block meets exactly 4: devices 0 to 4 form a chain of first blocks. In each block the positions follow a depth-first order of a token tree whose root is the block's first token: subtree_end[t] is the last in-block position of t's subtree, at least t's own position, and subtrees nest.
All inputs are finite; a program needn't handle non-finite values.
Results may differ from the reference program's by a relative error of at most 0.035.
Values may be sent and summed in bfloat16 or wider, within the bound.
No kernel may reach another device: no remote copies, remote signals or barrier semaphores. Data moves between devices by JAX's collectives and lax.ppermute only.
A program may use at most 64 MiB of HBM per device.

```python
import jax
import jax.numpy as jnp
from jax import lax

HQ = 32
KVH = 8
HD = 128
BLK = 256
DMAX = 4
BLK_DEV = 3
NB = 48
TOKENS = 12288


def draw_keys(key, part):
    key = jax.random.fold_in(key, 11)
    return jnp.clip(jax.random.normal(key, (TOKENS, KVH * HD), jnp.float32), -6.0, 6.0).astype(jnp.bfloat16)


def draw_queries(key, part):
    key = jax.random.fold_in(key, 23)
    return jnp.clip(jax.random.normal(key, (TOKENS, HQ * HD), jnp.float32), -6.0, 6.0).astype(jnp.bfloat16)


def draw_parent(key, part):
    key = jax.random.fold_in(key, 5)
    n_ctx = NB // BLK_DEV
    walk_key = jax.random.fold_in(key, 1)
    local_key = jax.random.fold_in(key, 2)
    draws = jax.random.randint(walk_key, (n_ctx,), 0, 1 << 20)

    def walk(carry, device):
        depth, upward = carry
        pick = draws[device] % jnp.maximum(device, 1)
        chosen = jnp.where(depth[pick] < DMAX, pick, upward[pick])
        above = jnp.where(device <= DMAX, device - 1, chosen)
        depth = depth.at[device].set(depth[above] + 1)
        upward = upward.at[device].set(above)
        return ((depth, upward), device)
    start = (jnp.zeros((n_ctx,), jnp.int32), jnp.full((n_ctx,), -1, jnp.int32))
    (depth, upward), _ = lax.scan(walk, start, jnp.arange(1, n_ctx, dtype=jnp.int32))
    index = jnp.arange(NB, dtype=jnp.int32)
    inner = index % BLK_DEV
    device = index // BLK_DEV
    local = device * BLK_DEV + jax.random.randint(local_key, (NB,), 0, 1 << 20) % jnp.maximum(inner, 1)
    local = jnp.where(inner == BLK_DEV - 1, index - 1, local)
    first = jnp.where(upward[device] >= 0, upward[device] * BLK_DEV, -1)
    return jnp.where(inner == 0, first, local).astype(jnp.int32)


def draw_subtree_end(key, part):
    key = jax.random.fold_in(key, 9)
    on_key = jax.random.fold_in(key, 1)
    size_key = jax.random.fold_in(key, 2)
    jumps_on = jax.random.randint(on_key, (BLK, NB), 0, 16) == 0
    jump_size = jax.random.randint(size_key, (BLK, NB), 1, 64)

    def advance(depth, inputs):
        on, size = inputs
        nxt = jnp.where(on, jnp.maximum(1, depth + 1 - size), depth + 1)
        return (nxt, nxt)
    _, rest = lax.scan(advance, jnp.zeros((NB,), jnp.int32), (jumps_on[1:], jump_size[1:]))
    depth = jnp.concatenate([jnp.zeros((1, NB), jnp.int32), rest], axis=0).T
    spots = jnp.arange(BLK, dtype=jnp.int32)
    later = spots[None, None, :] > spots[None, :, None]
    closes = later & (depth[:, None, :] <= depth[:, :, None])
    first = jnp.min(jnp.where(closes, spots[None, None, :], BLK), axis=2)
    return (first - 1).reshape(TOKENS).astype(jnp.int32)


def block_scale(own_key, dims, pieces, low, top_value):
    def one(dim, shards_of):
        heights = jax.random.uniform(jax.random.fold_in(jax.random.fold_in(own_key, 6), dim), (shards_of,), jnp.float32, low / len(pieces), top_value / len(pieces))
        return jnp.repeat(jnp.exp(heights), dims[dim] // shards_of).reshape((-1,) + (1,) * (len(dims) - dim - 1))

    loudness = one(*pieces[0])
    for cut in pieces[1:]:
        loudness = loudness * one(*cut)
    return loudness


def bell_draw(rng, shape, width, bound, split=(), held_as=jnp.bfloat16):
    level = block_scale(rng, shape, split, -0.22, 0.18) if split else 1.0
    drawn = jax.random.normal(rng, shape, jnp.float32) * width * level
    return jnp.minimum(jnp.maximum(drawn, -bound), bound).astype(held_as)


def setup_inputs(seed: int = 0) -> dict:
    key_list = jax.random.split(jax.random.key(seed), 7)
    return {
        "queries": draw_queries(jax.random.fold_in(key_list[6], 71), 0),
        "keys": draw_keys(jax.random.fold_in(key_list[6], 71), 0),
        "values": bell_draw(key_list[2], (TOKENS, KVH * HD), 1.0, 6.0, ((0, 128),)),
        "grad_out": bell_draw(key_list[3], (TOKENS, HQ * HD), 1.0, 6.0, ((0, 128),)),
        "parent": draw_parent(jax.random.fold_in(key_list[6], 71), 0),
        "subtree_end": draw_subtree_end(jax.random.fold_in(key_list[6], 71), 0),
    }


def chain_of(parent, start, steps):
    found = []
    current = start
    for _ in range(steps):
        current = jnp.where(current >= 0, parent[jnp.maximum(current, 0)], -1)
        found.append(current)
    return jnp.stack(found, axis=-1)


def reference(queries, keys, values, grad_out, parent, subtree_end):
    group = HQ // KVH
    scale = HD ** -0.5
    steps = BLK_DEV - 1 + DMAX
    kmax = steps + 1
    q_blocks = queries.reshape(NB, BLK, KVH, group, HD)
    g_blocks = grad_out.reshape(NB, BLK, KVH, group, HD)
    k_blocks = keys.reshape(NB, BLK, KVH, HD)
    v_blocks = values.reshape(NB, BLK, KVH, HD)
    e_blocks = subtree_end.reshape(NB, BLK)
    block_ids = jnp.arange(NB, dtype=jnp.int32)
    chains = chain_of(parent, block_ids, steps)
    positions = jnp.arange(BLK, dtype=jnp.int32)
    key_block = jnp.repeat(jnp.arange(kmax, dtype=jnp.int32), BLK)
    key_pos = jnp.tile(positions, kmax)

    def attend(carry, inputs):
        key_acc, value_acc = carry
        block_id, chain, q_blk, g_blk, ends = inputs
        ids = jnp.concatenate([block_id[None], chain]).astype(jnp.int32)
        safe = jnp.maximum(ids, 0)
        all_keys = k_blocks[safe].reshape(kmax * BLK, KVH, HD).astype(jnp.float32)
        all_values = v_blocks[safe].reshape(kmax * BLK, KVH, HD).astype(jnp.float32)
        tree = (key_pos[None, :] <= positions[:, None]) & (positions[:, None] <= ends[key_pos][None, :])
        valid = (ids >= 0)[key_block]
        allowed = jnp.where((key_block == 0)[None, :], tree, valid[None, :])
        q_f = q_blk.astype(jnp.float32)
        g_f = g_blk.astype(jnp.float32)
        scores = jnp.einsum("qkgd,nkd->kgqn", q_f, all_keys) * scale
        scores = jnp.where(allowed, scores, -1e30)
        peak = jnp.max(scores, axis=-1, keepdims=True)
        weights = jnp.exp(scores - peak)
        probs = weights / jnp.sum(weights, axis=-1, keepdims=True)
        probs_b = probs.astype(jnp.bfloat16)
        attended = jnp.einsum("kgqn,nkd->qkgd", probs_b.astype(jnp.float32), all_values).astype(jnp.bfloat16)
        dot_out = jnp.sum(g_f * attended.astype(jnp.float32), axis=-1).transpose(1, 2, 0)
        grad_probs = jnp.einsum("qkgd,nkd->kgqn", g_f, all_values)
        grad_scores = (probs * (grad_probs - dot_out[..., None])).astype(jnp.bfloat16)
        gs_f = grad_scores.astype(jnp.float32)
        q_grad = (jnp.einsum("kgqn,nkd->qkgd", gs_f, all_keys) * scale).astype(jnp.bfloat16)
        k_term = jnp.einsum("kgqn,qkgd->nkd", gs_f, q_f) * scale
        v_term = jnp.einsum("kgqn,qkgd->nkd", probs_b.astype(jnp.float32), g_f)
        key_acc = key_acc.at[safe].add(k_term.reshape(kmax, BLK, KVH, HD))
        value_acc = value_acc.at[safe].add(v_term.reshape(kmax, BLK, KVH, HD))
        return (key_acc, value_acc), (attended, q_grad)

    start = (jnp.zeros((NB, BLK, KVH, HD), jnp.float32), jnp.zeros((NB, BLK, KVH, HD), jnp.float32))
    (key_acc, value_acc), (outputs, q_grads) = lax.scan(attend, start, (block_ids, chains, q_blocks, g_blocks, e_blocks))
    attn_out = outputs.reshape(TOKENS, HQ * HD)
    grad_q = q_grads.reshape(TOKENS, HQ * HD)
    grad_k = key_acc.reshape(TOKENS, KVH * HD).astype(jnp.bfloat16)
    grad_v = value_acc.reshape(TOKENS, KVH * HD).astype(jnp.bfloat16)
    return (attn_out, grad_q, grad_k, grad_v)
```

```python
import functools

import jax
import jax.numpy as jnp
from jax import lax
from jax.experimental import pallas as pl
from jax.experimental.pallas import tpu as pltpu
from jax.sharding import PartitionSpec as P

HQ = 32
KVH = 8
HD = 128
BLK = 256
DMAX = 4
GROUP = HQ // KVH
SCALE = HD**-0.5
SCALE2 = SCALE * 1.4426950408889634
F32 = jnp.float32
BF16 = jnp.bfloat16


def dot(a, b, ca, cb):
    return lax.dot_general(a, b, (((ca,), (cb,)), ((), ())), preferred_element_type=F32)


def ancestor(here, blocks, parent, steps):
    current = here[0] * blocks
    for _ in range(steps):
        current = jnp.where(current >= 0, parent[jnp.maximum(current, 0)], -1)
    return current


def source(here, blocks, parent, steps):
    return jnp.maximum(ancestor(here, blocks, parent, steps), 0) // blocks


def attention_kernel(
    nb, here, parent, q_ref, g_ref, kv_ref, r0, r1, r2, r3, end_ref,
    o_ref, dq_ref, dkv_ref, terms_ref, ks, vs, dks, dvs, bias,
):
    h = pl.program_id(0)
    nr = DMAX * BLK
    found = [ancestor(here, nb, parent, j + 1) for j in range(DMAX)]

    @pl.when(h == 0)
    def _():
        for j, r in enumerate((r0, r1, r2, r3)):
            ks[j * BLK : (j + 1) * BLK] = r[0, :, :HD]
            vs[j * BLK : (j + 1) * BLK] = r[0, :, HD:]
        ks[nr:] = kv_ref[:, :HD]
        vs[nr:] = kv_ref[:, HD:]
        dks[...] = jnp.zeros_like(dks)
        dvs[...] = jnp.zeros_like(dvs)
        i = lax.broadcasted_iota(jnp.int32, (BLK, BLK), 0)
        p = lax.broadcasted_iota(jnp.int32, (BLK, BLK), 1)
        for b in range(nb):
            ok = (p <= i) & (i <= end_ref[b : b + 1, :])
            bias[b] = jnp.where(ok, 0.0, -1e30)

    for b in range(nb):
        rows = pl.ds(b * BLK, BLK)
        q = q_ref[rows, :]
        g = g_ref[rows, :]
        nk = nr + (b + 1) * BLK
        scores = dot(q, ks[:nk, :], 1, 1)
        parts = [scores[:, j * BLK : (j + 1) * BLK] for j in range(DMAX + b + 1)]
        parts[-1] = parts[-1] + bias[b]
        peak = None
        for j, x in enumerate(parts):
            t = jnp.maximum(x[:, :HD], x[:, HD:])
            if j < DMAX:
                t = jnp.where(found[j] >= 0, t, -3e38)
            peak = t if peak is None else jnp.maximum(peak, t)
        peak = jnp.max(peak, axis=1, keepdims=True)
        weights = []
        total = None
        for j, x in enumerate(parts):
            shift = jnp.where(found[j] >= 0, peak, 1e30) if j < DMAX else peak
            w = jnp.exp2((x - shift) * SCALE2)
            t = w[:, :HD] + w[:, HD:]
            total = t if total is None else total + t
            weights.append(w)
        inv = 1.0 / jnp.sum(total, axis=1, keepdims=True)
        w_b = jnp.concatenate([w.astype(BF16) for w in weights], axis=1)
        out = dot(w_b, vs[:nk, :], 1, 0) * inv
        o_ref[rows, :] = out.astype(BF16)
        g_b = (g.astype(F32) * inv).astype(BF16)
        dot_out = jnp.sum(g_b.astype(F32) * out, axis=1, keepdims=True)
        grad_probs = dot(g_b, vs[:nk, :], 1, 1)
        grad_scores = jnp.concatenate(
            [
                (weights[j] * (grad_probs[:, j * BLK : (j + 1) * BLK] - dot_out)).astype(BF16)
                for j in range(DMAX + b + 1)
            ],
            axis=1,
        )
        dq_ref[rows, :] = (dot(grad_scores, ks[:nk, :], 1, 0) * SCALE).astype(BF16)
        dks[:nk, :] += dot(grad_scores, q, 0, 0)
        dvs[:nk, :] += dot(w_b, g_b, 0, 0)

    @pl.when(h == GROUP - 1)
    def _():
        dkv_ref[:, :HD] = dks[nr:, :] * SCALE
        dkv_ref[:, HD:] = dvs[nr:, :]
        terms_ref[...] = jnp.zeros_like(terms_ref)
        for j in range(DMAX):

            @pl.when(found[j] >= 0)
            def _():
                at = found[j] // nb
                terms_ref[at, :, :HD] = (dks[j * BLK : (j + 1) * BLK, :] * SCALE).astype(BF16)
                terms_ref[at, :, HD:] = dvs[j * BLK : (j + 1) * BLK, :].astype(BF16)


def attention(here, parent, q, g, kv, arrived, ends):
    span = q.shape[0]
    nb = span // BLK
    n_ctx = arrived.shape[0]
    keys = (DMAX + nb) * BLK

    def whole(*shape):
        return pl.BlockSpec(shape, lambda h, here, parent: (0,) * len(shape))

    def above(steps):
        return pl.BlockSpec(
            (1, BLK, 2 * HD), lambda h, here, parent: (source(here, nb, parent, steps), 0, 0)
        )

    head = pl.BlockSpec((span, HD), lambda h, here, parent: (0, h))
    spec = pltpu.PrefetchScalarGridSpec(
        num_scalar_prefetch=2,
        grid=(GROUP,),
        in_specs=[head, head, whole(span, 2 * HD)]
        + [above(j + 1) for j in range(DMAX)]
        + [whole(nb, BLK)],
        out_specs=[head, head, whole(span, 2 * HD), whole(n_ctx, BLK, 2 * HD)],
        scratch_shapes=[
            pltpu.VMEM((keys, HD), BF16),
            pltpu.VMEM((keys, HD), BF16),
            pltpu.VMEM((keys, HD), F32),
            pltpu.VMEM((keys, HD), F32),
            pltpu.VMEM((nb, BLK, BLK), F32),
        ],
    )
    pairs = GROUP * sum(DMAX + b + 1 for b in range(nb)) * BLK * BLK
    return pl.pallas_call(
        functools.partial(attention_kernel, nb),
        grid_spec=spec,
        out_shape=[
            jax.ShapeDtypeStruct(q.shape, BF16),
            jax.ShapeDtypeStruct(q.shape, BF16),
            jax.ShapeDtypeStruct((span, 2 * HD), F32),
            jax.ShapeDtypeStruct((n_ctx, BLK, 2 * HD), BF16),
        ],
        compiler_params=pltpu.CompilerParams(vmem_limit_bytes=56 * 2**20),
        cost_estimate=pl.CostEstimate(
            flops=12 * pairs * HD, bytes_accessed=8 * span * 4 * HD, transcendentals=pairs
        ),
        name="tree_attention",
    )(here, parent, q, g, kv, arrived, arrived, arrived, arrived, ends)


def swap(x):
    return lax.all_to_all(x, "head", split_axis=0, concat_axis=0, tiled=True)


def local(queries, keys, values, grad_out, parent, subtree_end):
    n_head = lax.axis_size("head")
    n_ctx = lax.axis_size("ctx")
    here = lax.axis_index("ctx").astype(jnp.int32).reshape(1)
    rows = queries.shape[0]
    span = rows * n_head
    nb = span // BLK

    def split(x):
        return x.reshape(rows, n_head, -1)

    def by_head(x):
        return swap(x.transpose(1, 0, 2)).reshape(span, -1)

    kv = by_head(jnp.concatenate([split(keys), split(values)], axis=2))
    arrived = lax.all_gather(kv[:BLK], "ctx", axis=0, tiled=False)
    q = by_head(split(queries))
    g = by_head(split(grad_out))
    out, dq, dkv, terms = attention(here, parent, q, g, kv, arrived, subtree_end.reshape(nb, BLK))

    def by_token(x):
        return swap(x.reshape(n_head, rows, -1)).transpose(1, 0, 2)

    received = lax.all_to_all(terms, "ctx", split_axis=0, concat_axis=0, tiled=True)
    summed = jnp.sum(received.astype(F32), axis=0)
    dkv = jnp.concatenate([dkv[:BLK] + summed, dkv[BLK:]], axis=0).astype(BF16)
    attn_out = by_token(out).reshape(rows, -1)
    grad_q = by_token(dq).reshape(rows, -1)
    grads = by_token(dkv)
    return attn_out, grad_q, grads[:, :, :HD].reshape(rows, -1), grads[:, :, HD:].reshape(rows, -1)


def solution(mesh):
    placed = P(("ctx", "head"), None)
    return jax.shard_map(
        local,
        mesh=mesh,
        in_specs=(placed, placed, placed, placed, P(), P("ctx")),
        out_specs=(placed, placed, placed, placed),
        check_vma=False,
    )
```

```python
import functools

import jax
import jax.numpy as jnp
from jax import lax
from jax.experimental import pallas as pl
from jax.experimental.pallas import tpu as pltpu
from jax.sharding import PartitionSpec as P

HQ = 32
KVH = 8
HD = 128
BLK = 256
DMAX = 4
GROUP = HQ // KVH
SIDE = 4
SCALE = HD**-0.5
SCALE2 = SCALE * 1.4426950408889634
F32 = jnp.float32
BF16 = jnp.bfloat16


def dot(a, b, ca, cb):
    return lax.dot_general(a, b, (((ca,), (cb,)), ((), ())), preferred_element_type=F32)


def ring_pairs(side, cores, along, by):
    pairs = []
    for y in range(side):
        for z in range(side):
            for h in range(cores):
                if (along + h) % 2:
                    to = y * side + (z + by) % side
                else:
                    to = (y + by) % side * side + z
                pairs.append(((y * side + z) * cores + h, to * cores + h))
    return pairs


def shifted(x, along, by):
    pairs = ring_pairs(SIDE, lax.axis_size("head"), along, by)
    return lax.ppermute(x, ("ctx", "head"), pairs)


def offsets(here, device):
    dy = (here[0] // SIDE - device // SIDE) % SIDE
    dz = (here[0] % SIDE - device % SIDE) % SIDE
    odd = here[1] % 2 == 1
    return jnp.where(odd, dz, dy), jnp.where(odd, dy, dz)


def attention_kernel(
    nb, here, parent, q_ref, g_ref, kv_ref, a0, a1, a2, a3, end_ref,
    out_ref, dkv_ref, terms_ref, ks, vs, dks, dvs, bias,
):
    h = pl.program_id(0)
    nr = DMAX * BLK
    found = []
    current = here[0] * nb
    for _ in range(DMAX):
        current = jnp.where(current >= 0, parent[jnp.maximum(current, 0)], -1)
        found.append(current)

    @pl.when(h == 0)
    def _():
        for j in range(DMAX):
            second, first = offsets(here, jnp.maximum(found[j], 0) // nb)
            for s, r in enumerate((a0, a1, a2, a3)):

                @pl.when(second == s)
                def _():
                    ks[j * BLK : (j + 1) * BLK] = r[first, :, :HD]
                    vs[j * BLK : (j + 1) * BLK] = r[first, :, HD:]

        ks[nr:] = kv_ref[:, :HD]
        vs[nr:] = kv_ref[:, HD:]
        dks[...] = jnp.zeros_like(dks)
        dvs[...] = jnp.zeros_like(dvs)
        i = lax.broadcasted_iota(jnp.int32, (BLK, BLK), 0)
        p = lax.broadcasted_iota(jnp.int32, (BLK, BLK), 1)
        for b in range(nb):
            ok = (p <= i) & (i <= end_ref[b : b + 1, :])
            bias[b] = jnp.where(ok, 0.0, -1e30)

    for b in range(nb):
        rows = pl.ds(b * BLK, BLK)
        q = q_ref[rows, :]
        g = g_ref[rows, :]
        nk = nr + (b + 1) * BLK
        scores = dot(q, ks[:nk, :], 1, 1)
        parts = [scores[:, j * BLK : (j + 1) * BLK] for j in range(DMAX + b + 1)]
        parts[-1] = parts[-1] + bias[b]
        peak = None
        for j, x in enumerate(parts):
            t = jnp.maximum(x[:, :HD], x[:, HD:])
            if j < DMAX:
                t = jnp.where(found[j] >= 0, t, -3e38)
            peak = t if peak is None else jnp.maximum(peak, t)
        peak = jnp.max(peak, axis=1, keepdims=True)
        weights = []
        total = None
        for j, x in enumerate(parts):
            shift = jnp.where(found[j] >= 0, peak, 1e30) if j < DMAX else peak
            w = jnp.exp2((x - shift) * SCALE2)
            t = w[:, :HD] + w[:, HD:]
            total = t if total is None else total + t
            weights.append(w)
        inv = 1.0 / jnp.sum(total, axis=1, keepdims=True)
        w_b = jnp.concatenate([w.astype(BF16) for w in weights], axis=1)
        out = dot(w_b, vs[:nk, :], 1, 0) * inv
        out_ref[rows, pl.ds(pl.multiple_of(h * HD, HD), HD)] = out.astype(BF16)
        g_b = (g.astype(F32) * inv).astype(BF16)
        dot_out = jnp.sum(g_b.astype(F32) * out, axis=1, keepdims=True)
        grad_probs = dot(g_b, vs[:nk, :], 1, 1)
        grad_scores = jnp.concatenate(
            [
                (weights[j] * (grad_probs[:, j * BLK : (j + 1) * BLK] - dot_out)).astype(BF16)
                for j in range(DMAX + b + 1)
            ],
            axis=1,
        )
        dq = (dot(grad_scores, ks[:nk, :], 1, 0) * SCALE).astype(BF16)
        out_ref[rows, pl.ds(pl.multiple_of((GROUP + h) * HD, HD), HD)] = dq
        dks[:nk, :] += dot(grad_scores, q, 0, 0)
        dvs[:nk, :] += dot(w_b, g_b, 0, 0)

    @pl.when(h == GROUP - 1)
    def _():
        dkv_ref[:, :HD] = dks[nr:, :] * SCALE
        dkv_ref[:, HD:] = dvs[nr:, :]
        terms_ref[...] = jnp.zeros_like(terms_ref)
        for j in range(DMAX):

            @pl.when(found[j] >= 0)
            def _():
                second, first = offsets(here, found[j] // nb)
                at = (SIDE - second) % SIDE * SIDE + (SIDE - first) % SIDE
                terms_ref[at, :, :HD] = (dks[j * BLK : (j + 1) * BLK, :] * SCALE).astype(BF16)
                terms_ref[at, :, HD:] = dvs[j * BLK : (j + 1) * BLK, :].astype(BF16)


def attention(here, parent, qg, kv, arrived, ends):
    span = qg.shape[0]
    nb = span // BLK
    keys = (DMAX + nb) * BLK
    n_ctx = SIDE * SIDE

    def whole(*shape):
        return pl.BlockSpec(shape, lambda h, here, parent: (0,) * len(shape))

    spec = pltpu.PrefetchScalarGridSpec(
        num_scalar_prefetch=2,
        grid=(GROUP,),
        in_specs=[
            pl.BlockSpec((span, HD), lambda h, here, parent: (0, h)),
            pl.BlockSpec((span, HD), lambda h, here, parent: (0, GROUP + h)),
            whole(span, 2 * HD),
        ]
        + [whole(SIDE, BLK, 2 * HD)] * SIDE
        + [whole(nb, BLK)],
        out_specs=[
            whole(span, 2 * GROUP * HD),
            whole(span, 2 * HD),
            whole(n_ctx, BLK, 2 * HD),
        ],
        scratch_shapes=[
            pltpu.VMEM((keys, HD), BF16),
            pltpu.VMEM((keys, HD), BF16),
            pltpu.VMEM((keys, HD), F32),
            pltpu.VMEM((keys, HD), F32),
            pltpu.VMEM((nb, BLK, BLK), F32),
        ],
    )
    pairs = GROUP * sum(DMAX + b + 1 for b in range(nb)) * BLK * BLK
    return pl.pallas_call(
        functools.partial(attention_kernel, nb),
        grid_spec=spec,
        out_shape=[
            jax.ShapeDtypeStruct(qg.shape, BF16),
            jax.ShapeDtypeStruct((span, 2 * HD), F32),
            jax.ShapeDtypeStruct((n_ctx, BLK, 2 * HD), BF16),
        ],
        compiler_params=pltpu.CompilerParams(vmem_limit_bytes=56 * 2**20),
        cost_estimate=pl.CostEstimate(
            flops=12 * pairs * HD, bytes_accessed=8 * span * 4 * HD, transcendentals=pairs
        ),
        name="tree_attention",
    )(here, parent, qg, qg, kv, *arrived, ends)


def swap(x):
    return lax.all_to_all(x, "head", split_axis=0, concat_axis=0, tiled=True)


def local(queries, keys, values, grad_out, parent, subtree_end):
    n_head = lax.axis_size("head")
    here = jnp.stack([lax.axis_index("ctx"), lax.axis_index("head")]).astype(jnp.int32)
    rows = queries.shape[0]
    span = rows * n_head
    nb = span // BLK

    def by_head(x, y):
        both = [a.reshape(rows, n_head, -1) for a in (x, y)]
        return swap(jnp.concatenate(both, axis=2).transpose(1, 0, 2)).reshape(span, -1)

    kv = by_head(keys, values)
    first = kv[:BLK]
    line = jnp.stack([first] + [shifted(first, 1, s) for s in range(1, SIDE)])
    arrived = [line] + [shifted(line, 0, s) for s in range(1, SIDE)]
    qg = by_head(queries, grad_out)
    out, dkv, terms = attention(here, parent, qg, kv, arrived, subtree_end.reshape(nb, BLK))

    def send_back(x):
        return swap(x.reshape(n_head, rows, -1))

    def by_token(x):
        return [a.reshape(rows, -1) for a in jnp.split(x.transpose(1, 0, 2), 2, axis=2)]

    out = send_back(out)

    terms = terms.reshape(SIDE, SIDE, BLK, 2 * HD)
    part = terms[0].astype(F32)
    for s in range(1, SIDE):
        part = part + shifted(terms[s], 0, s).astype(F32)
    part_b = part.astype(BF16)
    summed = part[0]
    for s in range(1, SIDE):
        summed = summed + shifted(part_b[s], 1, s).astype(F32)
    dkv = jnp.concatenate([dkv[:BLK] + summed, dkv[BLK:]], axis=0).astype(BF16)
    out, dkv = lax.optimization_barrier((out, dkv))
    attn_out, grad_q = by_token(out)
    grad_k, grad_v = by_token(send_back(dkv))
    return attn_out, grad_q, grad_k, grad_v


def solution(mesh):
    placed = P(("ctx", "head"), None)
    return jax.shard_map(
        local,
        mesh=mesh,
        in_specs=(placed, placed, placed, placed, P(), P("ctx")),
        out_specs=(placed, placed, placed, placed),
        check_vma=False,
    )
```

```python
import functools

import jax
import jax.numpy as jnp
from jax import lax
from jax.experimental import pallas as pl
from jax.experimental.pallas import tpu as pltpu
from jax.sharding import PartitionSpec as P

HQ = 32
KVH = 8
HD = 128
BLK = 256
DMAX = 4
GROUP = HQ // KVH
SIDE = 4
SCALE = HD**-0.5
SCALE2 = SCALE * 1.4426950408889634
F32 = jnp.float32
BF16 = jnp.bfloat16


def dot(a, b, ca, cb):
    return lax.dot_general(a, b, (((ca,), (cb,)), ((), ())), preferred_element_type=F32)


def ring_pairs(side, cores, along, by):
    pairs = []
    for y in range(side):
        for z in range(side):
            for h in range(cores):
                if (along + h) % 2:
                    to = y * side + (z + by) % side
                else:
                    to = (y + by) % side * side + z
                pairs.append(((y * side + z) * cores + h, to * cores + h))
    return pairs


def shifted(x, along, by):
    pairs = ring_pairs(SIDE, lax.axis_size("head"), along, by)
    return lax.ppermute(x, ("ctx", "head"), pairs)


def offsets(here, device):
    dy = (here[0] // SIDE - device // SIDE) % SIDE
    dz = (here[0] % SIDE - device % SIDE) % SIDE
    odd = here[1] % 2 == 1
    return jnp.where(odd, dz, dy), jnp.where(odd, dy, dz)


def attention_kernel(
    nb, here, parent, q_ref, g_ref, kv_ref, a0, a1, a2, a3, end_ref,
    out_ref, dkv_ref, t0, t1, t2, t3, ks, vs, dks, dvs, bias,
):
    h = pl.program_id(0)
    nr = DMAX * BLK
    term_refs = (t0, t1, t2, t3)
    found = []
    current = here[0] * nb
    for _ in range(DMAX):
        current = jnp.where(current >= 0, parent[jnp.maximum(current, 0)], -1)
        found.append(current)

    @pl.when(h == 0)
    def _():
        for j in range(DMAX):
            second, first = offsets(here, jnp.maximum(found[j], 0) // nb)
            for s, r in enumerate((a0, a1, a2, a3)):

                @pl.when(second == s)
                def _():
                    ks[j * BLK : (j + 1) * BLK] = r[first, :, :HD]
                    vs[j * BLK : (j + 1) * BLK] = r[first, :, HD:]

        ks[nr:] = kv_ref[:, :HD]
        vs[nr:] = kv_ref[:, HD:]
        dks[...] = jnp.zeros_like(dks)
        dvs[...] = jnp.zeros_like(dvs)
        i = lax.broadcasted_iota(jnp.int32, (BLK, BLK), 0)
        p = lax.broadcasted_iota(jnp.int32, (BLK, BLK), 1)
        for b in range(nb):
            ok = (p <= i) & (i <= end_ref[b : b + 1, :])
            bias[b] = jnp.where(ok, 0.0, -1e30)

    def width(b):
        return nr + (b + 1) * BLK

    def block(ref, b):
        return ref[b * BLK : (b + 1) * BLK, :]

    def chunk(x, j):
        return x[:, j * BLK : (j + 1) * BLK]

    def scores(b):
        s = dot(block(q_ref, b), ks[: width(b), :], 1, 1)
        parts = [chunk(s, j) for j in range(DMAX + b + 1)]
        parts[-1] = parts[-1] + bias[b]
        peak = None
        for j, x in enumerate(parts):
            t = jnp.maximum(x[:, :HD], x[:, HD:])
            if j < DMAX:
                t = jnp.where(found[j] >= 0, t, -3e38)
            peak = t if peak is None else jnp.maximum(peak, t)
        return parts, peak

    def softmax(b, parts, peak):
        peak = jnp.max(peak, axis=1, keepdims=True)
        weights = []
        total = None
        for j, x in enumerate(parts):
            shift = jnp.where(found[j] >= 0, peak, 1e30) if j < DMAX else peak
            w = jnp.exp2((x - shift) * SCALE2)
            t = w[:, :HD] + w[:, HD:]
            total = t if total is None else total + t
            weights.append(w)
        return weights, total, jnp.concatenate([w.astype(BF16) for w in weights], axis=1)

    def attend(b, w_b, total):
        inv = 1.0 / jnp.sum(total, axis=1, keepdims=True)
        out = dot(w_b, vs[: width(b), :], 1, 0) * inv
        at = pl.ds(pl.multiple_of(h * HD, HD), HD)
        out_ref[b * BLK : (b + 1) * BLK, at] = out.astype(BF16)
        g_b = (block(g_ref, b).astype(F32) * inv).astype(BF16)
        return g_b, jnp.sum(g_b.astype(F32) * out, axis=1, keepdims=True)

    def grad_probs(b, g_b):
        return dot(g_b, vs[: width(b), :], 1, 1)

    def grad_scores(b, weights, grad_p, dot_out):
        each = [
            (weights[j] * (chunk(grad_p, j) - dot_out)).astype(BF16) for j in range(DMAX + b + 1)
        ]
        return jnp.concatenate(each, axis=1)

    def grads(b, grad_s, w_b, g_b):
        at = pl.ds(pl.multiple_of((GROUP + h) * HD, HD), HD)
        dq = dot(grad_s, ks[: width(b), :], 1, 0) * SCALE
        out_ref[b * BLK : (b + 1) * BLK, at] = dq.astype(BF16)
        dks[:, : width(b)] += dot(block(q_ref, b).T, grad_s, 1, 0)
        dvs[:, : width(b)] += dot(g_b.T, w_b, 1, 0)

    s, w, o, d, t = {}, {}, {}, {}, {}
    for step in range(nb + 3):
        b = step
        if b == 0:
            s[b] = scores(b)
        if b < nb:
            w[b] = softmax(b, *s.pop(b))
        if b + 1 < nb:
            s[b + 1] = scores(b + 1)
        if 0 <= b - 1 < nb:
            t[b - 1] = grad_scores(b - 1, w[b - 1][0], d.pop(b - 1), o[b - 1][1])
        if b < nb:
            o[b] = attend(b, w[b][2], w[b][1])
        if 0 <= b - 1 < nb:
            grads(b - 1, t.pop(b - 1), w[b - 1][2], o[b - 1][0])
        if b < nb:
            d[b] = grad_probs(b, o[b][0])

    @pl.when(h == GROUP - 1)
    def _():
        dk = dks[...].T * SCALE
        dv = dvs[...].T
        dkv_ref[:, :HD] = dk[nr:, :]
        dkv_ref[:, HD:] = dv[nr:, :]
        for r in term_refs:
            r[...] = jnp.zeros_like(r)
        for j in range(DMAX):
            second, first = offsets(here, jnp.maximum(found[j], 0) // nb)
            for s, r in enumerate(term_refs):

                @pl.when((found[j] >= 0) & ((SIDE - second) % SIDE == s))
                def _():
                    at = (SIDE - first) % SIDE
                    r[at, :, :HD] = dk[j * BLK : (j + 1) * BLK, :].astype(BF16)
                    r[at, :, HD:] = dv[j * BLK : (j + 1) * BLK, :].astype(BF16)


def attention(here, parent, qg, kv, arrived, ends):
    span = qg.shape[0]
    nb = span // BLK
    keys = (DMAX + nb) * BLK

    def whole(*shape):
        return pl.BlockSpec(shape, lambda h, here, parent: (0,) * len(shape))

    spec = pltpu.PrefetchScalarGridSpec(
        num_scalar_prefetch=2,
        grid=(GROUP,),
        in_specs=[
            pl.BlockSpec((span, HD), lambda h, here, parent: (0, h)),
            pl.BlockSpec((span, HD), lambda h, here, parent: (0, GROUP + h)),
            whole(span, 2 * HD),
        ]
        + [whole(SIDE, BLK, 2 * HD)] * SIDE
        + [whole(nb, BLK)],
        out_specs=[
            whole(span, 2 * GROUP * HD),
            whole(span, 2 * HD),
        ]
        + [whole(SIDE, BLK, 2 * HD)] * SIDE,
        scratch_shapes=[
            pltpu.VMEM((keys, HD), BF16),
            pltpu.VMEM((keys, HD), BF16),
            pltpu.VMEM((HD, keys), F32),
            pltpu.VMEM((HD, keys), F32),
            pltpu.VMEM((nb, BLK, BLK), F32),
        ],
    )
    pairs = GROUP * sum(DMAX + b + 1 for b in range(nb)) * BLK * BLK
    return pl.pallas_call(
        functools.partial(attention_kernel, nb),
        grid_spec=spec,
        out_shape=[
            jax.ShapeDtypeStruct(qg.shape, BF16),
            jax.ShapeDtypeStruct((span, 2 * HD), F32),
        ]
        + [jax.ShapeDtypeStruct((SIDE, BLK, 2 * HD), BF16)] * SIDE,
        compiler_params=pltpu.CompilerParams(vmem_limit_bytes=56 * 2**20),
        cost_estimate=pl.CostEstimate(
            flops=12 * pairs * HD, bytes_accessed=8 * span * 4 * HD, transcendentals=pairs
        ),
        name="tree_attention",
    )(here, parent, qg, qg, kv, *arrived, ends)


def swap(x):
    return lax.all_to_all(x, "head", split_axis=0, concat_axis=0, tiled=True)


def local(queries, keys, values, grad_out, parent, subtree_end):
    n_head = lax.axis_size("head")
    here = jnp.stack([lax.axis_index("ctx"), lax.axis_index("head")]).astype(jnp.int32)
    rows = queries.shape[0]
    span = rows * n_head
    nb = span // BLK

    def by_head(x, y):
        both = [a.reshape(rows, n_head, -1) for a in (x, y)]
        return swap(jnp.concatenate(both, axis=2).transpose(1, 0, 2)).reshape(span, -1)

    kv = by_head(keys, values)
    first = kv[:BLK]
    line = jnp.stack([first] + [shifted(first, 1, s) for s in range(1, SIDE)])
    arrived = [line] + [shifted(line, 0, s) for s in range(1, SIDE)]
    qg = by_head(queries, grad_out)
    out, dkv, *terms = attention(here, parent, qg, kv, arrived, subtree_end.reshape(nb, BLK))

    def send_back(x):
        return swap(x.reshape(n_head, rows, -1))

    def by_token(x):
        return [a.reshape(rows, -1) for a in jnp.split(x.transpose(1, 0, 2), 2, axis=2)]

    out = send_back(out)

    part = terms[0].astype(F32)
    for s in range(1, SIDE):
        part = part + shifted(terms[s], 0, s).astype(F32)
    part_b = part.astype(BF16)
    summed = part[0]
    for s in range(1, SIDE):
        summed = summed + shifted(part_b[s], 1, s).astype(F32)
    dkv = jnp.concatenate([dkv[:BLK] + summed, dkv[BLK:]], axis=0).astype(BF16)
    out, dkv = lax.optimization_barrier((out, dkv))
    attn_out, grad_q = by_token(out)
    grad_k, grad_v = by_token(send_back(dkv))
    return attn_out, grad_q, grad_k, grad_v


def solution(mesh):
    placed = P(("ctx", "head"), None)
    return jax.shard_map(
        local,
        mesh=mesh,
        in_specs=(placed, placed, placed, placed, P(), P("ctx")),
        out_specs=(placed, placed, placed, placed),
        check_vma=False,
    )
```

```python
import functools

import jax
import jax.numpy as jnp
from jax import lax
from jax.experimental import pallas as pl
from jax.experimental.pallas import tpu as pltpu
from jax.sharding import PartitionSpec as P

HQ = 32
KVH = 8
HD = 128
BLK = 256
DMAX = 4
GROUP = HQ // KVH
SIDE = 4
SCALE = HD**-0.5
SCALE2 = SCALE * 1.4426950408889634
F32 = jnp.float32
BF16 = jnp.bfloat16


def dot(a, b, ca, cb):
    return lax.dot_general(a, b, (((ca,), (cb,)), ((), ())), preferred_element_type=F32)


def ring_pairs(side, cores, along, by):
    pairs = []
    for y in range(side):
        for z in range(side):
            for h in range(cores):
                if (along + h) % 2:
                    to = y * side + (z + by) % side
                else:
                    to = (y + by) % side * side + z
                pairs.append(((y * side + z) * cores + h, to * cores + h))
    return pairs


def shifted(x, along, by):
    pairs = ring_pairs(SIDE, lax.axis_size("head"), along, by)
    return lax.ppermute(x, ("ctx", "head"), pairs)


def offsets(here, device):
    dy = (here[0] // SIDE - device // SIDE) % SIDE
    dz = (here[0] % SIDE - device % SIDE) % SIDE
    odd = here[1] % 2 == 1
    return jnp.where(odd, dz, dy), jnp.where(odd, dy, dz)


def attention_kernel(
    nb, here, parent, end_ref, qg_ref, kv_ref, a0, a1, a2, a3,
    out_ref, dfirst_ref, drest_ref, t0, t1, t2, t3,
    ks, vs, dks, dvs, bias, held, outs, terms, dfirst, drest, blank,
    kv_sem, in_sem, fetch_sem, out_sem, blank_sem, term_sem, rest_sem,
):
    nr = DMAX * BLK
    arrived = (a0, a1, a2, a3)
    term_refs = (t0, t1, t2, t3)
    found = []
    current = here[0] * nb
    for _ in range(DMAX):
        current = jnp.where(current >= 0, parent[jnp.maximum(current, 0)], -1)
        found.append(current)
    places = [offsets(here, jnp.maximum(f, 0) // nb) for f in found]

    def kv_copy(which):
        to = (ks, vs)[which].at[nr:, :]
        return pltpu.make_async_copy(kv_ref.at[:, which * HD : (which + 1) * HD], to, kv_sem.at[which])

    def fetch(j, r, at, which):
        to = (ks, vs)[which].at[j * BLK : (j + 1) * BLK, :]
        src = r.at[at, :, which * HD : (which + 1) * HD]
        return pltpu.make_async_copy(src, to, fetch_sem.at[j, which])

    def head_in(h, which):
        src = qg_ref.at[:, (which * GROUP + h) * HD : (which * GROUP + h + 1) * HD]
        return pltpu.make_async_copy(src, held.at[h, which], in_sem.at[h, which])

    def head_out(h, which):
        at = pl.ds(pl.multiple_of((which * GROUP + h) * HD, HD), HD)
        return pltpu.make_async_copy(outs.at[h, which], out_ref.at[:, at], out_sem.at[h, which])

    def blank_copy(s, at):
        return pltpu.make_async_copy(blank, term_refs[s].at[at], blank_sem.at[s * SIDE + at])

    for which in range(2):
        kv_copy(which).start()
        for j, (second, first) in enumerate(places):
            for s, r in enumerate(arrived):

                @pl.when(second == s)
                def _():
                    fetch(j, r, first, which).start()

        head_in(0, which).start()
    for h in range(1, GROUP):
        for which in range(2):
            head_in(h, which).start()
    i = lax.broadcasted_iota(jnp.int32, (BLK, BLK), 0)
    p = lax.broadcasted_iota(jnp.int32, (BLK, BLK), 1)
    for b in range(nb):
        ok = (p <= i) & (i <= end_ref[b : b + 1, :])
        bias[b] = jnp.where(ok, 0.0, -1e30)
    dks[...] = jnp.zeros_like(dks)
    dvs[...] = jnp.zeros_like(dvs)
    blank[...] = jnp.zeros_like(blank)
    for s in range(SIDE):
        for at in range(SIDE):
            blank_copy(s, at).start()
    for which in range(2):
        kv_copy(which).wait()
        for j in range(DMAX):
            fetch(j, a0, 0, which).wait()

    def width(b):
        return nr + (b + 1) * BLK

    def chunk(x, j):
        return x[:, j * BLK : (j + 1) * BLK]

    def one_head(h, carry):
        for which in range(2):
            pltpu.make_async_copy(
                qg_ref.at[:, :HD], held.at[h, which], in_sem.at[h, which]
            ).wait()

        def load(which, b):
            return held[h, which, b * BLK : (b + 1) * BLK, :]

        def store(which, b, x):
            outs[h, which, b * BLK : (b + 1) * BLK, :] = x.astype(BF16)

        def scores(n):
            b = n
            s = dot(load(0, n), ks[: width(b), :], 1, 1)
            parts = [chunk(s, j) for j in range(DMAX + b + 1)]
            parts[-1] = parts[-1] + bias[b]
            peak = None
            for j, x in enumerate(parts):
                t = jnp.maximum(x[:, :HD], x[:, HD:])
                if j < DMAX:
                    t = jnp.where(found[j] >= 0, t, -3e38)
                peak = t if peak is None else jnp.maximum(peak, t)
            return parts, peak

        def softmax(parts, peak):
            peak = jnp.max(peak, axis=1, keepdims=True)
            weights = []
            total = None
            for j, x in enumerate(parts):
                shift = jnp.where(found[j] >= 0, peak, 1e30) if j < DMAX else peak
                w = jnp.exp2((x - shift) * SCALE2)
                t = w[:, :HD] + w[:, HD:]
                total = t if total is None else total + t
                weights.append(w.astype(BF16))
            return weights, total, jnp.concatenate(weights, axis=1)

        def attend(n, w_b, total):
            inv = 1.0 / jnp.sum(total, axis=1, keepdims=True)
            out = dot(w_b, vs[: width(n), :], 1, 0) * inv
            store(0, n, out)
            g_b = (load(1, n).astype(F32) * inv).astype(BF16)
            return g_b, jnp.sum(g_b.astype(F32) * out, axis=1, keepdims=True)

        def grad_probs(n, g_b):
            return dot(g_b, vs[: width(n), :], 1, 1)

        def grad_scores(weights, grad_p, dot_out):
            each = [w * (chunk(grad_p, j) - dot_out).astype(BF16) for j, w in enumerate(weights)]
            return jnp.concatenate(each, axis=1)

        def grads(n, grad_s, w_b, g_b):
            keys = width(n)
            store(1, n, dot(grad_s, ks[:keys, :], 1, 0) * SCALE)
            dks[:, :keys] += dot(load(0, n).T, grad_s, 1, 0)
            dvs[:, :keys] += dot(g_b.T, w_b, 1, 0)

        s, w, o, d, t = {}, {}, {}, {}, {}
        s[0] = scores(0)
        for n in range(nb + 1):
            if n < nb:
                w[n] = softmax(*s.pop(n))
            if n + 1 < nb:
                s[n + 1] = scores(n + 1)
            if n >= 1:
                t[n - 1] = grad_scores(w[n - 1][0], d.pop(n - 1), o[n - 1][1])
            if n < nb:
                o[n] = attend(n, w[n][2], w[n][1])
            if n >= 1:
                grads(n - 1, t.pop(n - 1), w.pop(n - 1)[2], o.pop(n - 1)[0])
            if n < nb:
                d[n] = grad_probs(n, o[n][0])
        for which in range(2):
            head_out(h, which).start()
        return carry

    lax.fori_loop(0, GROUP, one_head, 0)
    for s in range(SIDE):
        for at in range(SIDE):
            blank_copy(s, at).wait()
    dk = dks[:, :nr].T * SCALE
    dv = dvs[:, :nr].T
    for j, (second, first) in enumerate(places):
        terms[j, :, :HD] = dk[j * BLK : (j + 1) * BLK, :].astype(BF16)
        terms[j, :, HD:] = dv[j * BLK : (j + 1) * BLK, :].astype(BF16)
        for s, r in enumerate(term_refs):

            @pl.when((found[j] >= 0) & ((SIDE - second) % SIDE == s))
            def _():
                at = (SIDE - first) % SIDE
                pltpu.make_async_copy(terms.at[j], r.at[at], term_sem.at[j]).start()

    dk = dks[:, nr:].T * SCALE
    dv = dvs[:, nr:].T
    dfirst[:, :HD] = dk[:BLK, :]
    dfirst[:, HD:] = dv[:BLK, :]
    drest[:, :HD] = dk[BLK:, :].astype(BF16)
    drest[:, HD:] = dv[BLK:, :].astype(BF16)
    last = (
        pltpu.make_async_copy(dfirst, dfirst_ref, rest_sem.at[0]),
        pltpu.make_async_copy(drest, drest_ref, rest_sem.at[1]),
    )
    for c in last:
        c.start()
    for h in range(GROUP):
        for which in range(2):
            head_out(h, which).wait()
    for j in range(DMAX):

        @pl.when(found[j] >= 0)
        def _():
            pltpu.make_async_copy(terms.at[j], t0.at[0], term_sem.at[j]).wait()

    for c in last:
        c.wait()


def attention(here, parent, qg, kv, arrived, ends):
    span = qg.shape[0]
    nb = span // BLK
    keys = (DMAX + nb) * BLK

    anywhere = pl.BlockSpec(memory_space=pl.ANY)
    spec = pltpu.PrefetchScalarGridSpec(
        num_scalar_prefetch=2,
        grid=(),
        in_specs=[pl.BlockSpec(memory_space=pltpu.VMEM)] + [anywhere] * (2 + SIDE),
        out_specs=[anywhere] * (3 + SIDE),
        scratch_shapes=[
            pltpu.VMEM((keys, HD), BF16),
            pltpu.VMEM((keys, HD), BF16),
            pltpu.VMEM((HD, keys), F32),
            pltpu.VMEM((HD, keys), F32),
            pltpu.VMEM((nb, BLK, BLK), F32),
            pltpu.VMEM((GROUP, 2, span, HD), BF16),
            pltpu.VMEM((GROUP, 2, span, HD), BF16),
            pltpu.VMEM((DMAX, BLK, 2 * HD), BF16),
            pltpu.VMEM((BLK, 2 * HD), F32),
            pltpu.VMEM((span - BLK, 2 * HD), BF16),
            pltpu.VMEM((BLK, 2 * HD), BF16),
            pltpu.SemaphoreType.DMA((2,)),
            pltpu.SemaphoreType.DMA((GROUP, 2)),
            pltpu.SemaphoreType.DMA((DMAX, 2)),
            pltpu.SemaphoreType.DMA((GROUP, 2)),
            pltpu.SemaphoreType.DMA((SIDE * SIDE,)),
            pltpu.SemaphoreType.DMA((DMAX,)),
            pltpu.SemaphoreType.DMA((2,)),
        ],
    )
    pairs = GROUP * sum(DMAX + b + 1 for b in range(nb)) * BLK * BLK
    return pl.pallas_call(
        functools.partial(attention_kernel, nb),
        grid_spec=spec,
        out_shape=[
            jax.ShapeDtypeStruct(qg.shape, BF16),
            jax.ShapeDtypeStruct((BLK, 2 * HD), F32),
            jax.ShapeDtypeStruct((span - BLK, 2 * HD), BF16),
        ]
        + [jax.ShapeDtypeStruct((SIDE, BLK, 2 * HD), BF16)] * SIDE,
        compiler_params=pltpu.CompilerParams(vmem_limit_bytes=24 * 2**20),
        cost_estimate=pl.CostEstimate(
            flops=12 * pairs * HD, bytes_accessed=8 * span * 4 * HD, transcendentals=pairs
        ),
        name="tree_attention",
    )(here, parent, ends, qg, kv, *arrived)


def swap(x):
    return lax.all_to_all(x, "head", split_axis=0, concat_axis=0, tiled=True)


def local(queries, keys, values, grad_out, parent, subtree_end):
    n_head = lax.axis_size("head")
    here = jnp.stack([lax.axis_index("ctx"), lax.axis_index("head")]).astype(jnp.int32)
    rows = queries.shape[0]
    span = rows * n_head
    nb = span // BLK

    def by_head(x, y):
        both = [a.reshape(rows, n_head, -1) for a in (x, y)]
        return swap(jnp.concatenate(both, axis=2).transpose(1, 0, 2)).reshape(span, -1)

    kv = by_head(keys, values)
    first = kv[:BLK]
    line = jnp.stack([first] + [shifted(first, 1, s) for s in range(1, SIDE)])
    arrived = [line] + [shifted(line, 0, s) for s in range(1, SIDE)]
    qg = by_head(queries, grad_out)
    out, dfirst, drest, *terms = attention(here, parent, qg, kv, arrived, subtree_end.reshape(nb, BLK))

    def send_back(x):
        return swap(x.reshape(n_head, rows, -1))

    def by_token(x):
        return [a.reshape(rows, -1) for a in jnp.split(x.transpose(1, 0, 2), 2, axis=2)]

    out = send_back(out)

    got = [terms[0]] + [shifted(terms[s], 0, s) for s in range(1, SIDE)]
    summed = sum(x[0].astype(F32) for x in got)
    part = sum(x[1:].astype(F32) for x in got).astype(BF16)
    for s in range(1, SIDE):
        summed = summed + shifted(part[s - 1], 1, s).astype(F32)
    dkv = jnp.concatenate([(dfirst + summed).astype(BF16), drest], axis=0)
    out, dkv = lax.optimization_barrier((out, dkv))
    attn_out, grad_q = by_token(out)
    grad_k, grad_v = by_token(send_back(dkv))
    return attn_out, grad_q, grad_k, grad_v


def solution(mesh):
    placed = P(("ctx", "head"), None)
    return jax.shard_map(
        local,
        mesh=mesh,
        in_specs=(placed, placed, placed, placed, P(), P("ctx")),
        out_specs=(placed, placed, placed, placed),
        check_vma=False,
    )
```

```python
import functools

import jax
import jax.numpy as jnp
from jax import lax
from jax.experimental import pallas as pl
from jax.experimental.pallas import tpu as pltpu
from jax.sharding import PartitionSpec as P

HQ = 32
KVH = 8
HD = 128
BLK = 256
DMAX = 4
GROUP = HQ // KVH
SIDE = 4
SCALE = HD**-0.5
SCALE2 = SCALE * 1.4426950408889634
F32 = jnp.float32
BF16 = jnp.bfloat16


def dot(a, b, ca, cb):
    return lax.dot_general(a, b, (((ca,), (cb,)), ((), ())), preferred_element_type=F32)


def ring_pairs(side, cores, along, by):
    pairs = []
    for y in range(side):
        for z in range(side):
            for h in range(cores):
                if (along + h) % 2:
                    to = y * side + (z + by) % side
                else:
                    to = (y + by) % side * side + z
                pairs.append(((y * side + z) * cores + h, to * cores + h))
    return pairs


def shifted(x, along, by):
    pairs = ring_pairs(SIDE, lax.axis_size("head"), along, by)
    return lax.ppermute(x, ("ctx", "head"), pairs)


def offsets(here, device):
    dy = (here[0] // SIDE - device // SIDE) % SIDE
    dz = (here[0] % SIDE - device % SIDE) % SIDE
    odd = here[1] % 2 == 1
    return jnp.where(odd, dz, dy), jnp.where(odd, dy, dz)


def attention_kernel(
    nb, here, parent, end_ref, qg_ref, kv_ref, a0, a1, a2, a3,
    out_ref, dfirst_ref, drest_ref, t0, t1, t2, t3,
    ks, vs, dks, dvs, bias, held, outs, terms, dfirst, drest, blank,
    kv_sem, in_sem, fetch_sem, out_sem, blank_sem, term_sem, rest_sem,
):
    nr = DMAX * BLK
    arrived = (a0, a1, a2, a3)
    term_refs = (t0, t1, t2, t3)
    found = []
    current = here[0] * nb
    for _ in range(DMAX):
        current = jnp.where(current >= 0, parent[jnp.maximum(current, 0)], -1)
        found.append(current)
    places = [offsets(here, jnp.maximum(f, 0) // nb) for f in found]

    def kv_copy(which):
        to = (ks, vs)[which].at[nr:, :]
        return pltpu.make_async_copy(kv_ref.at[:, which * HD : (which + 1) * HD], to, kv_sem.at[which])

    def fetch(j, r, at, which):
        to = (ks, vs)[which].at[j * BLK : (j + 1) * BLK, :]
        src = r.at[at, :, which * HD : (which + 1) * HD]
        return pltpu.make_async_copy(src, to, fetch_sem.at[j, which])

    def head_in(h, which):
        src = qg_ref.at[:, (which * GROUP + h) * HD : (which * GROUP + h + 1) * HD]
        return pltpu.make_async_copy(src, held.at[h, which], in_sem.at[h, which])

    def head_out(h, which):
        at = pl.ds(pl.multiple_of((which * GROUP + h) * HD, HD), HD)
        return pltpu.make_async_copy(outs.at[h, which], out_ref.at[:, at], out_sem.at[h, which])

    def blank_copy(s, at):
        return pltpu.make_async_copy(blank, term_refs[s].at[at], blank_sem.at[s * SIDE + at])

    for which in range(2):
        kv_copy(which).start()
        for j, (second, first) in enumerate(places):
            for s, r in enumerate(arrived):

                @pl.when(second == s)
                def _():
                    fetch(j, r, first, which).start()

        head_in(0, which).start()
    for h in range(1, GROUP):
        for which in range(2):
            head_in(h, which).start()
    i = lax.broadcasted_iota(jnp.int32, (BLK, BLK), 0)
    p = lax.broadcasted_iota(jnp.int32, (BLK, BLK), 1)
    for b in range(nb):
        ok = (p <= i) & (i <= end_ref[b : b + 1, :])
        bias[b] = jnp.where(ok, 0.0, -1e30)
    dks[...] = jnp.zeros_like(dks)
    dvs[...] = jnp.zeros_like(dvs)
    blank[...] = jnp.zeros_like(blank)
    for s in range(SIDE):
        for at in range(SIDE):
            blank_copy(s, at).start()
    for which in range(2):
        kv_copy(which).wait()
        for j in range(DMAX):
            fetch(j, a0, 0, which).wait()

    def width(b):
        return nr + (b + 1) * BLK

    def chunk(x, j):
        return x[:, j * BLK : (j + 1) * BLK]

    def one_head(h, carry):
        for which in range(2):
            pltpu.make_async_copy(
                qg_ref.at[:, :HD], held.at[h, which], in_sem.at[h, which]
            ).wait()

        def load(which, b):
            return held[h, which, b * BLK : (b + 1) * BLK, :]

        def store(which, b, x):
            outs[h, which, b * BLK : (b + 1) * BLK, :] = x.astype(BF16)

        def scores(n):
            b = n
            s = dot(load(0, n), ks[: width(b), :], 1, 1)
            parts = [chunk(s, j) for j in range(DMAX + b + 1)]
            parts[-1] = parts[-1] + bias[b]
            peak = None
            for j, x in enumerate(parts):
                t = jnp.maximum(x[:, :HD], x[:, HD:])
                if j < DMAX:
                    t = jnp.where(found[j] >= 0, t, -3e38)
                peak = t if peak is None else jnp.maximum(peak, t)
            return parts, peak

        def softmax(parts, peak):
            peak = jnp.max(peak, axis=1, keepdims=True)
            weights = []
            total = None
            for j, x in enumerate(parts):
                shift = jnp.where(found[j] >= 0, peak, 1e30) if j < DMAX else peak
                w = jnp.exp2((x - shift) * SCALE2)
                t = w[:, :HD] + w[:, HD:]
                total = t if total is None else total + t
                weights.append(w.astype(BF16))
            return weights, total, jnp.concatenate(weights, axis=1)

        def attend(n, w_b, total):
            inv = 1.0 / jnp.sum(total, axis=1, keepdims=True)
            out = dot(w_b, vs[: width(n), :], 1, 0) * inv
            store(0, n, out)
            g_b = (load(1, n).astype(F32) * inv).astype(BF16)
            return g_b, jnp.sum(g_b.astype(F32) * out, axis=1, keepdims=True)

        def grad_probs(n, g_b):
            return dot(g_b, vs[: width(n), :], 1, 1)

        def grad_scores(weights, grad_p, dot_out):
            each = [w * (chunk(grad_p, j) - dot_out).astype(BF16) for j, w in enumerate(weights)]
            return jnp.concatenate(each, axis=1)

        def grads(n, grad_s, w_b, g_b):
            keys = width(n)
            store(1, n, dot(grad_s, ks[:keys, :], 1, 0) * SCALE)
            dks[:, :keys] += dot(load(0, n).T, grad_s, 1, 0)
            dvs[:, :keys] += dot(g_b.T, w_b, 1, 0)

        s, w, o, d, t = {}, {}, {}, {}, {}
        s[0] = scores(0)
        for n in range(nb + 1):
            if n < nb:
                w[n] = softmax(*s.pop(n))
            if n + 1 < nb:
                s[n + 1] = scores(n + 1)
            if n >= 1:
                t[n - 1] = grad_scores(w[n - 1][0], d.pop(n - 1), o[n - 1][1])
            if n < nb:
                o[n] = attend(n, w[n][2], w[n][1])
            if n >= 1:
                grads(n - 1, t.pop(n - 1), w.pop(n - 1)[2], o.pop(n - 1)[0])
            if n < nb:
                d[n] = grad_probs(n, o[n][0])
        for which in range(2):
            head_out(h, which).start()
        return carry

    lax.fori_loop(0, GROUP, one_head, 0)
    for s in range(SIDE):
        for at in range(SIDE):
            blank_copy(s, at).wait()
    dk = dks[:, :nr].T * SCALE
    dv = dvs[:, :nr].T
    for j, (second, first) in enumerate(places):
        terms[j, :, :HD] = dk[j * BLK : (j + 1) * BLK, :].astype(BF16)
        terms[j, :, HD:] = dv[j * BLK : (j + 1) * BLK, :].astype(BF16)
        for s, r in enumerate(term_refs):

            @pl.when((found[j] >= 0) & ((SIDE - second) % SIDE == s))
            def _():
                at = (SIDE - first) % SIDE
                pltpu.make_async_copy(terms.at[j], r.at[at], term_sem.at[j]).start()

    dk = dks[:, nr:].T * SCALE
    dv = dvs[:, nr:].T
    dfirst[:, :HD] = dk[:BLK, :]
    dfirst[:, HD:] = dv[:BLK, :]
    drest[:, :HD] = dk[BLK:, :].astype(BF16)
    drest[:, HD:] = dv[BLK:, :].astype(BF16)
    last = (
        pltpu.make_async_copy(dfirst, dfirst_ref, rest_sem.at[0]),
        pltpu.make_async_copy(drest, drest_ref, rest_sem.at[1]),
    )
    for c in last:
        c.start()
    for h in range(GROUP):
        for which in range(2):
            head_out(h, which).wait()
    for j in range(DMAX):

        @pl.when(found[j] >= 0)
        def _():
            pltpu.make_async_copy(terms.at[j], t0.at[0], term_sem.at[j]).wait()

    for c in last:
        c.wait()


def attention(here, parent, qg, kv, arrived, ends):
    span = qg.shape[0]
    nb = span // BLK
    keys = (DMAX + nb) * BLK

    anywhere = pl.BlockSpec(memory_space=pl.ANY)
    spec = pltpu.PrefetchScalarGridSpec(
        num_scalar_prefetch=2,
        grid=(),
        in_specs=[pl.BlockSpec(memory_space=pltpu.VMEM)] + [anywhere] * (2 + SIDE),
        out_specs=[anywhere] * (3 + SIDE),
        scratch_shapes=[
            pltpu.VMEM((keys, HD), BF16),
            pltpu.VMEM((keys, HD), BF16),
            pltpu.VMEM((HD, keys), F32),
            pltpu.VMEM((HD, keys), F32),
            pltpu.VMEM((nb, BLK, BLK), F32),
            pltpu.VMEM((GROUP, 2, span, HD), BF16),
            pltpu.VMEM((GROUP, 2, span, HD), BF16),
            pltpu.VMEM((DMAX, BLK, 2 * HD), BF16),
            pltpu.VMEM((BLK, 2 * HD), F32),
            pltpu.VMEM((span - BLK, 2 * HD), BF16),
            pltpu.VMEM((BLK, 2 * HD), BF16),
            pltpu.SemaphoreType.DMA((2,)),
            pltpu.SemaphoreType.DMA((GROUP, 2)),
            pltpu.SemaphoreType.DMA((DMAX, 2)),
            pltpu.SemaphoreType.DMA((GROUP, 2)),
            pltpu.SemaphoreType.DMA((SIDE * SIDE,)),
            pltpu.SemaphoreType.DMA((DMAX,)),
            pltpu.SemaphoreType.DMA((2,)),
        ],
    )
    pairs = GROUP * sum(DMAX + b + 1 for b in range(nb)) * BLK * BLK
    return pl.pallas_call(
        functools.partial(attention_kernel, nb),
        grid_spec=spec,
        out_shape=[
            jax.ShapeDtypeStruct(qg.shape, BF16),
            jax.ShapeDtypeStruct((BLK, 2 * HD), F32),
            jax.ShapeDtypeStruct((span - BLK, 2 * HD), BF16),
        ]
        + [jax.ShapeDtypeStruct((SIDE, BLK, 2 * HD), BF16)] * SIDE,
        compiler_params=pltpu.CompilerParams(vmem_limit_bytes=24 * 2**20),
        cost_estimate=pl.CostEstimate(
            flops=12 * pairs * HD, bytes_accessed=8 * span * 4 * HD, transcendentals=pairs
        ),
        name="tree_attention",
    )(here, parent, ends, qg, kv, *arrived)


def swap(x):
    return lax.all_to_all(x, "head", split_axis=0, concat_axis=0, tiled=True)


def local(queries, keys, values, grad_out, parent, subtree_end):
    n_head = lax.axis_size("head")
    here = jnp.stack([lax.axis_index("ctx"), lax.axis_index("head")]).astype(jnp.int32)
    rows = queries.shape[0]
    span = rows * n_head
    nb = span // BLK

    def by_head(x, y):
        both = [a.reshape(rows, n_head, -1) for a in (x, y)]
        return swap(jnp.concatenate(both, axis=2).transpose(1, 0, 2)).reshape(span, -1)

    kv = by_head(keys, values)
    first = kv[:BLK]
    by = {s: shifted(first, 1, s) for s in (2, 1, 3)}
    line = jnp.stack([first] + [by[s] for s in range(1, SIDE)])
    by = {s: shifted(line, 0, s) for s in (2, 1, 3)}
    arrived = [line] + [by[s] for s in range(1, SIDE)]
    qg = by_head(queries, grad_out)
    out, dfirst, drest, *terms = attention(here, parent, qg, kv, arrived, subtree_end.reshape(nb, BLK))

    def send_back(x):
        return swap(x.reshape(n_head, rows, -1))

    def by_token(x):
        return [a.reshape(rows, -1) for a in jnp.split(x.transpose(1, 0, 2), 2, axis=2)]

    out = send_back(out)

    by = {s: shifted(terms[s], 0, s) for s in (2, 1, 3)}
    got = [terms[0]] + [by[s] for s in range(1, SIDE)]
    own = lax.optimization_barrier(dfirst + sum(x[0].astype(F32) for x in got))
    part = sum(x[1:].astype(F32) for x in got).astype(BF16)
    for s in (2, 1, 3):
        own = own + shifted(part[s - 1], 1, s).astype(F32)
    dkv = jnp.concatenate([own.astype(BF16), drest], axis=0)
    out, dkv = lax.optimization_barrier((out, dkv))
    attn_out, grad_q = by_token(out)
    grad_k, grad_v = by_token(send_back(dkv))
    return attn_out, grad_q, grad_k, grad_v


def solution(mesh):
    placed = P(("ctx", "head"), None)
    return jax.shard_map(
        local,
        mesh=mesh,
        in_specs=(placed, placed, placed, placed, P(), P("ctx")),
        out_specs=(placed, placed, placed, placed),
        check_vma=False,
    )
```

```python
import functools

import jax
import jax.numpy as jnp
from jax import lax
from jax.experimental import pallas as pl
from jax.experimental.pallas import tpu as pltpu
from jax.sharding import PartitionSpec as P

HQ = 32
KVH = 8
HD = 128
BLK = 256
DMAX = 4
GROUP = HQ // KVH
SIDE = 4
SCALE = HD**-0.5
SCALE2 = SCALE * 1.4426950408889634
F32 = jnp.float32
BF16 = jnp.bfloat16


def dot(a, b, ca, cb):
    return lax.dot_general(a, b, (((ca,), (cb,)), ((), ())), preferred_element_type=F32)


def ring_pairs(side, cores, along, by, up):
    pairs = []
    for y in range(side):
        for z in range(side):
            for h in range(cores):
                if (along + h) % 2:
                    to = y * side + (z + by) % side
                else:
                    to_y = (y + by) % side
                    if up and 2 * by == side == 4 and to_y < y:
                        to_y = (0, 1)[to_y == 0]
                    to = to_y * side + z
                pairs.append(((y * side + z) * cores + h, to * cores + h))
    return pairs


def shifted(x, along, by, up):
    pairs = ring_pairs(SIDE, lax.axis_size("head"), along, by, up)
    return lax.ppermute(x, ("ctx", "head"), pairs)


def offsets(here, device):
    dy = (here[0] // SIDE - device // SIDE) % SIDE
    dz = (here[0] % SIDE - device % SIDE) % SIDE
    odd = here[1] % 2 == 1
    return jnp.where(odd, dz, dy), jnp.where(odd, dy, dz)


def attention_kernel(
    nb, here, parent, end_ref, qg_ref, kv_ref, a0, a1, a2, a3,
    out_ref, dfirst_ref, drest_ref, t0, t1, t2, t3,
    ks, vs, dks, dvs, bias, held, outs, terms, dfirst, drest, blank,
    kv_sem, in_sem, fetch_sem, out_sem, blank_sem, term_sem, rest_sem,
):
    nr = DMAX * BLK
    arrived = (a0, a1, a2, a3)
    term_refs = (t0, t1, t2, t3)
    found = []
    current = here[0] * nb
    for _ in range(DMAX):
        current = jnp.where(current >= 0, parent[jnp.maximum(current, 0)], -1)
        found.append(current)
    places = [offsets(here, jnp.maximum(f, 0) // nb) for f in found]

    def kv_copy(which):
        to = (ks, vs)[which].at[nr:, :]
        return pltpu.make_async_copy(kv_ref.at[:, which * HD : (which + 1) * HD], to, kv_sem.at[which])

    def fetch(j, r, at, which):
        to = (ks, vs)[which].at[j * BLK : (j + 1) * BLK, :]
        src = r.at[at, :, which * HD : (which + 1) * HD]
        return pltpu.make_async_copy(src, to, fetch_sem.at[j, which])

    def head_in(h, which):
        src = qg_ref.at[:, (which * GROUP + h) * HD : (which * GROUP + h + 1) * HD]
        return pltpu.make_async_copy(src, held.at[h, which], in_sem.at[h, which])

    def head_out(h, which):
        at = pl.ds(pl.multiple_of((which * GROUP + h) * HD, HD), HD)
        return pltpu.make_async_copy(outs.at[h, which], out_ref.at[:, at], out_sem.at[h, which])

    def blank_copy(s, at):
        return pltpu.make_async_copy(blank, term_refs[s].at[at], blank_sem.at[s * SIDE + at])

    for which in range(2):
        kv_copy(which).start()
        for j, (second, first) in enumerate(places):
            for s, r in enumerate(arrived):

                @pl.when(second == s)
                def _():
                    fetch(j, r, first, which).start()

        head_in(0, which).start()
    for h in range(1, GROUP):
        for which in range(2):
            head_in(h, which).start()
    i = lax.broadcasted_iota(jnp.int32, (BLK, BLK), 0)
    p = lax.broadcasted_iota(jnp.int32, (BLK, BLK), 1)
    for b in range(nb):
        ok = (p <= i) & (i <= end_ref[b : b + 1, :])
        bias[b] = jnp.where(ok, 0.0, -1e30)
    dks[...] = jnp.zeros_like(dks)
    dvs[...] = jnp.zeros_like(dvs)
    blank[...] = jnp.zeros_like(blank)
    for s in range(SIDE):
        for at in range(SIDE):
            blank_copy(s, at).start()
    for which in range(2):
        kv_copy(which).wait()
        for j in range(DMAX):
            fetch(j, a0, 0, which).wait()

    def width(b):
        return nr + (b + 1) * BLK

    def chunk(x, j):
        return x[:, j * BLK : (j + 1) * BLK]

    def one_head(h, carry):
        for which in range(2):
            pltpu.make_async_copy(
                qg_ref.at[:, :HD], held.at[h, which], in_sem.at[h, which]
            ).wait()

        def load(which, b):
            return held[h, which, b * BLK : (b + 1) * BLK, :]

        def store(which, b, x):
            outs[h, which, b * BLK : (b + 1) * BLK, :] = x.astype(BF16)

        def scores(n):
            b = n
            s = dot(load(0, n), ks[: width(b), :], 1, 1)
            parts = [chunk(s, j) for j in range(DMAX + b + 1)]
            parts[-1] = parts[-1] + bias[b]
            peak = None
            for j, x in enumerate(parts):
                t = jnp.maximum(x[:, :HD], x[:, HD:])
                if j < DMAX:
                    t = jnp.where(found[j] >= 0, t, -3e38)
                peak = t if peak is None else jnp.maximum(peak, t)
            return parts, peak

        def softmax(parts, peak):
            peak = jnp.max(peak, axis=1, keepdims=True)
            weights = []
            total = None
            for j, x in enumerate(parts):
                shift = jnp.where(found[j] >= 0, peak, 1e30) if j < DMAX else peak
                w = jnp.exp2((x - shift) * SCALE2)
                t = w[:, :HD] + w[:, HD:]
                total = t if total is None else total + t
                weights.append(w.astype(BF16))
            return weights, total, jnp.concatenate(weights, axis=1)

        def attend(n, w_b, total):
            inv = 1.0 / jnp.sum(total, axis=1, keepdims=True)
            out = dot(w_b, vs[: width(n), :], 1, 0) * inv
            store(0, n, out)
            g_b = (load(1, n).astype(F32) * inv).astype(BF16)
            return g_b, jnp.sum(g_b.astype(F32) * out, axis=1, keepdims=True)

        def grad_probs(n, g_b):
            return dot(g_b, vs[: width(n), :], 1, 1)

        def grad_scores(weights, grad_p, dot_out):
            each = [w * (chunk(grad_p, j) - dot_out).astype(BF16) for j, w in enumerate(weights)]
            return jnp.concatenate(each, axis=1)

        def grads(n, grad_s, w_b, g_b):
            keys = width(n)
            store(1, n, dot(grad_s, ks[:keys, :], 1, 0) * SCALE)
            dks[:, :keys] += dot(load(0, n).T, grad_s, 1, 0)
            dvs[:, :keys] += dot(g_b.T, w_b, 1, 0)

        s, w, o, d, t = {}, {}, {}, {}, {}
        s[0] = scores(0)
        for n in range(nb + 1):
            if n < nb:
                w[n] = softmax(*s.pop(n))
            if n + 1 < nb:
                s[n + 1] = scores(n + 1)
            if n >= 1:
                t[n - 1] = grad_scores(w[n - 1][0], d.pop(n - 1), o[n - 1][1])
            if n < nb:
                o[n] = attend(n, w[n][2], w[n][1])
            if n >= 1:
                grads(n - 1, t.pop(n - 1), w.pop(n - 1)[2], o.pop(n - 1)[0])
            if n < nb:
                d[n] = grad_probs(n, o[n][0])
        for which in range(2):
            head_out(h, which).start()
        return carry

    lax.fori_loop(0, GROUP, one_head, 0)
    for s in range(SIDE):
        for at in range(SIDE):
            blank_copy(s, at).wait()
    dk = dks[:, :nr].T * SCALE
    dv = dvs[:, :nr].T
    for j, (second, first) in enumerate(places):
        terms[j, :, :HD] = dk[j * BLK : (j + 1) * BLK, :].astype(BF16)
        terms[j, :, HD:] = dv[j * BLK : (j + 1) * BLK, :].astype(BF16)
        for s, r in enumerate(term_refs):

            @pl.when((found[j] >= 0) & ((SIDE - second) % SIDE == s))
            def _():
                at = (SIDE - first) % SIDE
                pltpu.make_async_copy(terms.at[j], r.at[at], term_sem.at[j]).start()

    dk = dks[:, nr:].T * SCALE
    dv = dvs[:, nr:].T
    dfirst[:, :HD] = dk[:BLK, :]
    dfirst[:, HD:] = dv[:BLK, :]
    drest[:, :HD] = dk[BLK:, :].astype(BF16)
    drest[:, HD:] = dv[BLK:, :].astype(BF16)
    last = (
        pltpu.make_async_copy(dfirst, dfirst_ref, rest_sem.at[0]),
        pltpu.make_async_copy(drest, drest_ref, rest_sem.at[1]),
    )
    for c in last:
        c.start()
    for h in range(GROUP):
        for which in range(2):
            head_out(h, which).wait()
    for j in range(DMAX):

        @pl.when(found[j] >= 0)
        def _():
            pltpu.make_async_copy(terms.at[j], t0.at[0], term_sem.at[j]).wait()

    for c in last:
        c.wait()


def attention(here, parent, qg, kv, arrived, ends):
    span = qg.shape[0]
    nb = span // BLK
    keys = (DMAX + nb) * BLK

    anywhere = pl.BlockSpec(memory_space=pl.ANY)
    spec = pltpu.PrefetchScalarGridSpec(
        num_scalar_prefetch=2,
        grid=(),
        in_specs=[pl.BlockSpec(memory_space=pltpu.VMEM)] + [anywhere] * (2 + SIDE),
        out_specs=[anywhere] * (3 + SIDE),
        scratch_shapes=[
            pltpu.VMEM((keys, HD), BF16),
            pltpu.VMEM((keys, HD), BF16),
            pltpu.VMEM((HD, keys), F32),
            pltpu.VMEM((HD, keys), F32),
            pltpu.VMEM((nb, BLK, BLK), F32),
            pltpu.VMEM((GROUP, 2, span, HD), BF16),
            pltpu.VMEM((GROUP, 2, span, HD), BF16),
            pltpu.VMEM((DMAX, BLK, 2 * HD), BF16),
            pltpu.VMEM((BLK, 2 * HD), F32),
            pltpu.VMEM((span - BLK, 2 * HD), BF16),
            pltpu.VMEM((BLK, 2 * HD), BF16),
            pltpu.SemaphoreType.DMA((2,)),
            pltpu.SemaphoreType.DMA((GROUP, 2)),
            pltpu.SemaphoreType.DMA((DMAX, 2)),
            pltpu.SemaphoreType.DMA((GROUP, 2)),
            pltpu.SemaphoreType.DMA((SIDE * SIDE,)),
            pltpu.SemaphoreType.DMA((DMAX,)),
            pltpu.SemaphoreType.DMA((2,)),
        ],
    )
    pairs = GROUP * sum(DMAX + b + 1 for b in range(nb)) * BLK * BLK
    return pl.pallas_call(
        functools.partial(attention_kernel, nb),
        grid_spec=spec,
        out_shape=[
            jax.ShapeDtypeStruct(qg.shape, BF16),
            jax.ShapeDtypeStruct((BLK, 2 * HD), F32),
            jax.ShapeDtypeStruct((span - BLK, 2 * HD), BF16),
        ]
        + [jax.ShapeDtypeStruct((SIDE, BLK, 2 * HD), BF16)] * SIDE,
        compiler_params=pltpu.CompilerParams(vmem_limit_bytes=24 * 2**20),
        cost_estimate=pl.CostEstimate(
            flops=12 * pairs * HD, bytes_accessed=8 * span * 4 * HD, transcendentals=pairs
        ),
        name="tree_attention",
    )(here, parent, ends, qg, kv, *arrived)


def swap(x):
    return lax.all_to_all(x, "head", split_axis=0, concat_axis=0, tiled=True)


def local(queries, keys, values, grad_out, parent, subtree_end):
    n_head = lax.axis_size("head")
    here = jnp.stack([lax.axis_index("ctx"), lax.axis_index("head")]).astype(jnp.int32)
    rows = queries.shape[0]
    span = rows * n_head
    nb = span // BLK

    def by_head(x, y):
        both = [a.reshape(rows, n_head, -1) for a in (x, y)]
        return swap(jnp.concatenate(both, axis=2).transpose(1, 0, 2)).reshape(span, -1)

    kv = by_head(keys, values)
    first = kv[:BLK]
    by = {s: shifted(first, 1, s, True) for s in (2, 1, 3)}
    line = jnp.stack([first] + [by[s] for s in range(1, SIDE)])
    by = {s: shifted(line, 0, s, True) for s in (2, 1, 3)}
    arrived = [line] + [by[s] for s in range(1, SIDE)]
    qg = by_head(queries, grad_out)
    out, dfirst, drest, *terms = attention(here, parent, qg, kv, arrived, subtree_end.reshape(nb, BLK))

    def send_back(x):
        return swap(x.reshape(n_head, rows, -1))

    def by_token(x):
        return [a.reshape(rows, -1) for a in jnp.split(x.transpose(1, 0, 2), 2, axis=2)]

    out = send_back(out)

    by = {s: shifted(terms[s], 0, s, False) for s in (2, 1, 3)}
    got = [terms[0]] + [by[s] for s in range(1, SIDE)]
    own = lax.optimization_barrier(dfirst + sum(x[0].astype(F32) for x in got))
    part = sum(x[1:].astype(F32) for x in got).astype(BF16)
    for s in (2, 1, 3):
        own = own + shifted(part[s - 1], 1, s, False).astype(F32)
    dkv = jnp.concatenate([own.astype(BF16), drest], axis=0)
    out, dkv = lax.optimization_barrier((out, dkv))
    attn_out, grad_q = by_token(out)
    grad_k, grad_v = by_token(send_back(dkv))
    return attn_out, grad_q, grad_k, grad_v


def solution(mesh):
    placed = P(("ctx", "head"), None)
    return jax.shard_map(
        local,
        mesh=mesh,
        in_specs=(placed, placed, placed, placed, P(), P("ctx")),
        out_specs=(placed, placed, placed, placed),
        check_vma=False,
    )
```

```python
import functools

import jax
import jax.numpy as jnp
from jax import lax
from jax.experimental import pallas as pl
from jax.experimental.pallas import tpu as pltpu
from jax.sharding import PartitionSpec as P

HQ = 32
KVH = 8
HD = 128
BLK = 256
DMAX = 4
GROUP = HQ // KVH
SIDE = 4
SCALE = HD**-0.5
SCALE2 = SCALE * 1.4426950408889634
F32 = jnp.float32
BF16 = jnp.bfloat16


def dot(a, b, ca, cb):
    return lax.dot_general(a, b, (((ca,), (cb,)), ((), ())), preferred_element_type=F32)


def ring_pairs(side, cores, along, by, up):
    pairs = []
    for y in range(side):
        for z in range(side):
            for h in range(cores):
                if (along + h) % 2:
                    to = y * side + (z + by) % side
                else:
                    to_y = (y + by) % side
                    if 2 * by == side == 4 and (to_y < y) == up:
                        to_y = to_y ^ 1
                    to = to_y * side + z
                pairs.append(((y * side + z) * cores + h, to * cores + h))
    return pairs


def shifted(x, along, by, up):
    pairs = ring_pairs(SIDE, lax.axis_size("head"), along, by, up)
    return lax.ppermute(x, ("ctx", "head"), pairs)


def offsets(here, device):
    dy = (here[0] // SIDE - device // SIDE) % SIDE
    dz = (here[0] % SIDE - device % SIDE) % SIDE
    odd = here[1] % 2 == 1
    return jnp.where(odd, dz, dy), jnp.where(odd, dy, dz)


def attention_kernel(
    nb, here, parent, end_ref, qg_ref, kv_ref, a0, a1, a2, a3,
    out_ref, dfirst_ref, drest_ref, t0, t1, t2, t3,
    ks, vs, dks, dvs, bias, held, outs, terms, dfirst, drest, blank,
    kv_sem, in_sem, fetch_sem, out_sem, blank_sem, term_sem, rest_sem,
):
    nr = DMAX * BLK
    arrived = (a0, a1, a2, a3)
    term_refs = (t0, t1, t2, t3)
    found = []
    current = here[0] * nb
    for _ in range(DMAX):
        current = jnp.where(current >= 0, parent[jnp.maximum(current, 0)], -1)
        found.append(current)
    places = [offsets(here, jnp.maximum(f, 0) // nb) for f in found]

    def kv_copy(which):
        to = (ks, vs)[which].at[nr:, :]
        return pltpu.make_async_copy(kv_ref.at[:, which * HD : (which + 1) * HD], to, kv_sem.at[which])

    def fetch(j, r, at, which):
        to = (ks, vs)[which].at[j * BLK : (j + 1) * BLK, :]
        src = r.at[at, :, which * HD : (which + 1) * HD]
        return pltpu.make_async_copy(src, to, fetch_sem.at[j, which])

    def head_in(h, which):
        src = qg_ref.at[:, (which * GROUP + h) * HD : (which * GROUP + h + 1) * HD]
        return pltpu.make_async_copy(src, held.at[h, which], in_sem.at[h, which])

    def head_out(h, which):
        at = pl.ds(pl.multiple_of((which * GROUP + h) * HD, HD), HD)
        return pltpu.make_async_copy(outs.at[h, which], out_ref.at[:, at], out_sem.at[h, which])

    def blank_copy(s, at):
        return pltpu.make_async_copy(blank, term_refs[s].at[at], blank_sem.at[s * SIDE + at])

    for which in range(2):
        kv_copy(which).start()
        for j, (second, first) in enumerate(places):
            for s, r in enumerate(arrived):

                @pl.when(second == s)
                def _():
                    fetch(j, r, first, which).start()

        head_in(0, which).start()
    for h in range(1, GROUP):
        for which in range(2):
            head_in(h, which).start()
    i = lax.broadcasted_iota(jnp.int32, (BLK, BLK), 0)
    p = lax.broadcasted_iota(jnp.int32, (BLK, BLK), 1)
    for b in range(nb):
        ok = (p <= i) & (i <= end_ref[b : b + 1, :])
        bias[b] = jnp.where(ok, 0.0, -1e30)
    dks[...] = jnp.zeros_like(dks)
    dvs[...] = jnp.zeros_like(dvs)
    blank[...] = jnp.zeros_like(blank)
    for s in range(SIDE):
        for at in range(SIDE):
            blank_copy(s, at).start()
    for which in range(2):
        kv_copy(which).wait()
        for j in range(DMAX):
            fetch(j, a0, 0, which).wait()

    def width(b):
        return nr + (b + 1) * BLK

    def chunk(x, j):
        return x[:, j * BLK : (j + 1) * BLK]

    def one_head(h, carry):
        for which in range(2):
            pltpu.make_async_copy(
                qg_ref.at[:, :HD], held.at[h, which], in_sem.at[h, which]
            ).wait()

        def load(which, b):
            return held[h, which, b * BLK : (b + 1) * BLK, :]

        def store(which, b, x):
            outs[h, which, b * BLK : (b + 1) * BLK, :] = x.astype(BF16)

        def scores(n):
            b = n
            s = dot(load(0, n), ks[: width(b), :], 1, 1)
            parts = [chunk(s, j) for j in range(DMAX + b + 1)]
            parts[-1] = parts[-1] + bias[b]
            peak = None
            for j, x in enumerate(parts):
                t = jnp.maximum(x[:, :HD], x[:, HD:])
                if j < DMAX:
                    t = jnp.where(found[j] >= 0, t, -3e38)
                peak = t if peak is None else jnp.maximum(peak, t)
            return parts, peak

        def softmax(parts, peak):
            peak = jnp.max(peak, axis=1, keepdims=True)
            weights = []
            total = None
            for j, x in enumerate(parts):
                shift = jnp.where(found[j] >= 0, peak, 1e30) if j < DMAX else peak
                w = jnp.exp2((x - shift) * SCALE2)
                t = w[:, :HD] + w[:, HD:]
                total = t if total is None else total + t
                weights.append(w.astype(BF16))
            return weights, total, jnp.concatenate(weights, axis=1)

        def attend(n, w_b, total):
            inv = 1.0 / jnp.sum(total, axis=1, keepdims=True)
            out = dot(w_b, vs[: width(n), :], 1, 0) * inv
            store(0, n, out)
            g_b = (load(1, n).astype(F32) * inv).astype(BF16)
            return g_b, jnp.sum(g_b.astype(F32) * out, axis=1, keepdims=True)

        def grad_probs(n, g_b):
            return dot(g_b, vs[: width(n), :], 1, 1)

        def grad_scores(weights, grad_p, dot_out):
            each = [w * (chunk(grad_p, j) - dot_out).astype(BF16) for j, w in enumerate(weights)]
            return jnp.concatenate(each, axis=1)

        def grads(n, grad_s, w_b, g_b):
            keys = width(n)
            store(1, n, dot(grad_s, ks[:keys, :], 1, 0) * SCALE)
            dks[:, :keys] += dot(load(0, n).T, grad_s, 1, 0)
            dvs[:, :keys] += dot(g_b.T, w_b, 1, 0)

        s, w, o, d, t = {}, {}, {}, {}, {}
        s[0] = scores(0)
        for n in range(nb + 1):
            if n < nb:
                w[n] = softmax(*s.pop(n))
            if n + 1 < nb:
                s[n + 1] = scores(n + 1)
            if n >= 1:
                t[n - 1] = grad_scores(w[n - 1][0], d.pop(n - 1), o[n - 1][1])
            if n < nb:
                o[n] = attend(n, w[n][2], w[n][1])
            if n >= 1:
                grads(n - 1, t.pop(n - 1), w.pop(n - 1)[2], o.pop(n - 1)[0])
            if n < nb:
                d[n] = grad_probs(n, o[n][0])
        for which in range(2):
            head_out(h, which).start()
        return carry

    lax.fori_loop(0, GROUP, one_head, 0)
    for s in range(SIDE):
        for at in range(SIDE):
            blank_copy(s, at).wait()
    dk = dks[:, :nr].T * SCALE
    dv = dvs[:, :nr].T
    for j, (second, first) in enumerate(places):
        terms[j, :, :HD] = dk[j * BLK : (j + 1) * BLK, :].astype(BF16)
        terms[j, :, HD:] = dv[j * BLK : (j + 1) * BLK, :].astype(BF16)
        for s, r in enumerate(term_refs):

            @pl.when((found[j] >= 0) & ((SIDE - second) % SIDE == s))
            def _():
                at = (SIDE - first) % SIDE
                pltpu.make_async_copy(terms.at[j], r.at[at], term_sem.at[j]).start()

    dk = dks[:, nr:].T * SCALE
    dv = dvs[:, nr:].T
    dfirst[:, :HD] = dk[:BLK, :]
    dfirst[:, HD:] = dv[:BLK, :]
    drest[:, :HD] = dk[BLK:, :].astype(BF16)
    drest[:, HD:] = dv[BLK:, :].astype(BF16)
    last = (
        pltpu.make_async_copy(dfirst, dfirst_ref, rest_sem.at[0]),
        pltpu.make_async_copy(drest, drest_ref, rest_sem.at[1]),
    )
    for c in last:
        c.start()
    for h in range(GROUP):
        for which in range(2):
            head_out(h, which).wait()
    for j in range(DMAX):

        @pl.when(found[j] >= 0)
        def _():
            pltpu.make_async_copy(terms.at[j], t0.at[0], term_sem.at[j]).wait()

    for c in last:
        c.wait()


def attention(here, parent, qg, kv, arrived, ends):
    span = qg.shape[0]
    nb = span // BLK
    keys = (DMAX + nb) * BLK

    anywhere = pl.BlockSpec(memory_space=pl.ANY)
    spec = pltpu.PrefetchScalarGridSpec(
        num_scalar_prefetch=2,
        grid=(),
        in_specs=[pl.BlockSpec(memory_space=pltpu.VMEM)] + [anywhere] * (2 + SIDE),
        out_specs=[anywhere] * (3 + SIDE),
        scratch_shapes=[
            pltpu.VMEM((keys, HD), BF16),
            pltpu.VMEM((keys, HD), BF16),
            pltpu.VMEM((HD, keys), F32),
            pltpu.VMEM((HD, keys), F32),
            pltpu.VMEM((nb, BLK, BLK), F32),
            pltpu.VMEM((GROUP, 2, span, HD), BF16),
            pltpu.VMEM((GROUP, 2, span, HD), BF16),
            pltpu.VMEM((DMAX, BLK, 2 * HD), BF16),
            pltpu.VMEM((BLK, 2 * HD), F32),
            pltpu.VMEM((span - BLK, 2 * HD), BF16),
            pltpu.VMEM((BLK, 2 * HD), BF16),
            pltpu.SemaphoreType.DMA((2,)),
            pltpu.SemaphoreType.DMA((GROUP, 2)),
            pltpu.SemaphoreType.DMA((DMAX, 2)),
            pltpu.SemaphoreType.DMA((GROUP, 2)),
            pltpu.SemaphoreType.DMA((SIDE * SIDE,)),
            pltpu.SemaphoreType.DMA((DMAX,)),
            pltpu.SemaphoreType.DMA((2,)),
        ],
    )
    pairs = GROUP * sum(DMAX + b + 1 for b in range(nb)) * BLK * BLK
    return pl.pallas_call(
        functools.partial(attention_kernel, nb),
        grid_spec=spec,
        out_shape=[
            jax.ShapeDtypeStruct(qg.shape, BF16),
            jax.ShapeDtypeStruct((BLK, 2 * HD), F32),
            jax.ShapeDtypeStruct((span - BLK, 2 * HD), BF16),
        ]
        + [jax.ShapeDtypeStruct((SIDE, BLK, 2 * HD), BF16)] * SIDE,
        compiler_params=pltpu.CompilerParams(vmem_limit_bytes=24 * 2**20),
        cost_estimate=pl.CostEstimate(
            flops=12 * pairs * HD, bytes_accessed=8 * span * 4 * HD, transcendentals=pairs
        ),
        name="tree_attention",
    )(here, parent, ends, qg, kv, *arrived)


def swap(x):
    return lax.all_to_all(x, "head", split_axis=0, concat_axis=0, tiled=True)


def local(queries, keys, values, grad_out, parent, subtree_end):
    n_head = lax.axis_size("head")
    here = jnp.stack([lax.axis_index("ctx"), lax.axis_index("head")]).astype(jnp.int32)
    rows = queries.shape[0]
    span = rows * n_head
    nb = span // BLK

    def by_head(x, y):
        both = [a.reshape(rows, n_head, -1) for a in (x, y)]
        return swap(jnp.concatenate(both, axis=2).transpose(1, 0, 2)).reshape(span, -1)

    kv = by_head(keys, values)
    first = kv[:BLK]
    by = {s: shifted(first, 1, s, True) for s in (2, 1, 3)}
    line = jnp.stack([first] + [by[s] for s in range(1, SIDE)])
    by = {s: shifted(line, 0, s, True) for s in (2, 1, 3)}
    arrived = [line] + [by[s] for s in range(1, SIDE)]
    qg = by_head(queries, grad_out)
    out, dfirst, drest, *terms = attention(here, parent, qg, kv, arrived, subtree_end.reshape(nb, BLK))

    def send_back(x):
        return swap(x.reshape(n_head, rows, -1))

    def by_token(x):
        return [a.reshape(rows, -1) for a in jnp.split(x.transpose(1, 0, 2), 2, axis=2)]

    out = send_back(out)

    by = {s: shifted(terms[s], 0, s, False) for s in (2, 1, 3)}
    got = [terms[0]] + [by[s] for s in range(1, SIDE)]
    own = lax.optimization_barrier(dfirst + sum(x[0].astype(F32) for x in got))
    part = sum(x[1:].astype(F32) for x in got).astype(BF16)
    for s in (2, 1, 3):
        own = own + shifted(part[s - 1], 1, s, False).astype(F32)
    dkv = jnp.concatenate([own.astype(BF16), drest], axis=0)
    out, dkv = lax.optimization_barrier((out, dkv))
    attn_out, grad_q = by_token(out)
    grad_k, grad_v = by_token(send_back(dkv))
    return attn_out, grad_q, grad_k, grad_v


def solution(mesh):
    placed = P(("ctx", "head"), None)
    return jax.shard_map(
        local,
        mesh=mesh,
        in_specs=(placed, placed, placed, placed, P(), P("ctx")),
        out_specs=(placed, placed, placed, placed),
        check_vma=False,
    )
```

```python
import functools

import jax
import jax.numpy as jnp
from jax import lax
from jax.experimental import pallas as pl
from jax.experimental.pallas import tpu as pltpu
from jax.sharding import PartitionSpec as P

HQ = 32
KVH = 8
HD = 128
BLK = 256
DMAX = 4
GROUP = HQ // KVH
SIDE = 4
SCALE = HD**-0.5
SCALE2 = SCALE * 1.4426950408889634
F32 = jnp.float32
BF16 = jnp.bfloat16


def dot(a, b, ca, cb):
    return lax.dot_general(a, b, (((ca,), (cb,)), ((), ())), preferred_element_type=F32)


def ring_pairs(side, cores, along, by, up):
    pairs = []
    for y in range(side):
        for z in range(side):
            for h in range(cores):
                if (along + h) % 2:
                    to = y * side + (z + by) % side
                else:
                    to_y = (y + by) % side
                    if 2 * by == side == 4 and (to_y < y) == up:
                        to_y = to_y ^ 1
                    to = to_y * side + z
                pairs.append(((y * side + z) * cores + h, to * cores + h))
    return pairs


def shifted(x, along, by, up):
    pairs = ring_pairs(SIDE, lax.axis_size("head"), along, by, up)
    return lax.ppermute(x, ("ctx", "head"), pairs)


def offsets(here, device):
    dy = (here[0] // SIDE - device // SIDE) % SIDE
    dz = (here[0] % SIDE - device % SIDE) % SIDE
    odd = here[1] % 2 == 1
    return jnp.where(odd, dz, dy), jnp.where(odd, dy, dz)


def attention_kernel(
    nb, here, parent, end_ref, qg_ref, kv_ref, a0, a1, a2, a3,
    out_ref, dfirst_ref, drest_ref, t0, t1, t2, t3,
    ks, vs, dks, dvs, bias, held, outs, terms, dfirst, drest, blank,
    kv_sem, in_sem, fetch_sem, out_sem, blank_sem, term_sem, rest_sem,
):
    nr = DMAX * BLK
    arrived = (a0, a1, a2, a3)
    term_refs = (t0, t1, t2, t3)
    found = []
    current = here[0] * nb
    for _ in range(DMAX):
        current = jnp.where(current >= 0, parent[jnp.maximum(current, 0)], -1)
        found.append(current)
    places = [offsets(here, jnp.maximum(f, 0) // nb) for f in found]

    def kv_copy(which):
        to = (ks, vs)[which].at[nr:, :]
        return pltpu.make_async_copy(kv_ref.at[:, which * HD : (which + 1) * HD], to, kv_sem.at[which])

    def fetch(j, r, at, which):
        to = (ks, vs)[which].at[j * BLK : (j + 1) * BLK, :]
        src = r.at[at, :, which * HD : (which + 1) * HD]
        return pltpu.make_async_copy(src, to, fetch_sem.at[j, which])

    def head_in(h, which):
        src = qg_ref.at[:, (which * GROUP + h) * HD : (which * GROUP + h + 1) * HD]
        return pltpu.make_async_copy(src, held.at[h, which], in_sem.at[h, which])

    def head_out(h, which):
        at = pl.ds(pl.multiple_of((which * GROUP + h) * HD, HD), HD)
        return pltpu.make_async_copy(outs.at[h, which], out_ref.at[:, at], out_sem.at[h, which])

    def blank_copy(s, at):
        return pltpu.make_async_copy(blank, term_refs[s].at[at], blank_sem.at[s * SIDE + at])

    for which in range(2):
        kv_copy(which).start()
        for j, (second, first) in enumerate(places):
            for s, r in enumerate(arrived):

                @pl.when(second == s)
                def _():
                    fetch(j, r, first, which).start()

        head_in(0, which).start()
    for h in range(1, GROUP):
        for which in range(2):
            head_in(h, which).start()
    i = lax.broadcasted_iota(jnp.int32, (BLK, BLK), 0)
    p = lax.broadcasted_iota(jnp.int32, (BLK, BLK), 1)
    for b in range(nb):
        ok = (p <= i) & (i <= end_ref[b : b + 1, :])
        bias[b] = jnp.where(ok, 0.0, -1e30)
    dks[...] = jnp.zeros_like(dks)
    dvs[...] = jnp.zeros_like(dvs)
    blank[...] = jnp.zeros_like(blank)
    for s in range(SIDE):
        for at in range(SIDE):
            blank_copy(s, at).start()
    for which in range(2):
        kv_copy(which).wait()
        for j in range(DMAX):
            fetch(j, a0, 0, which).wait()

    def width(b):
        return nr + (b + 1) * BLK

    def chunk(x, j):
        return x[:, j * BLK : (j + 1) * BLK]

    def one_head(h, carry):
        for which in range(2):
            pltpu.make_async_copy(
                qg_ref.at[:, :HD], held.at[h, which], in_sem.at[h, which]
            ).wait()

        def load(which, b):
            return held[h, which, b * BLK : (b + 1) * BLK, :]

        def store(which, b, x):
            outs[h, which, b * BLK : (b + 1) * BLK, :] = x.astype(BF16)

        def scores(n):
            b = n
            s = dot(load(0, n), ks[: width(b), :], 1, 1)
            parts = [chunk(s, j) for j in range(DMAX + b + 1)]
            parts[-1] = parts[-1] + bias[b]
            peak = None
            for j, x in enumerate(parts):
                t = jnp.maximum(x[:, :HD], x[:, HD:])
                if j < DMAX:
                    t = jnp.where(found[j] >= 0, t, -3e38)
                peak = t if peak is None else jnp.maximum(peak, t)
            return parts, peak

        def softmax(parts, peak):
            peak = jnp.max(peak, axis=1, keepdims=True)
            weights = []
            total = None
            for j, x in enumerate(parts):
                shift = jnp.where(found[j] >= 0, peak, 1e30) if j < DMAX else peak
                w = jnp.exp2((x - shift) * SCALE2)
                t = w[:, :HD] + w[:, HD:]
                total = t if total is None else total + t
                weights.append(w.astype(BF16))
            return weights, total, jnp.concatenate(weights, axis=1)

        def attend(n, w_b, total):
            inv = 1.0 / jnp.sum(total, axis=1, keepdims=True)
            out = dot(w_b, vs[: width(n), :], 1, 0) * inv
            store(0, n, out)
            g_b = (load(1, n).astype(F32) * inv).astype(BF16)
            return g_b, jnp.sum(g_b.astype(F32) * out, axis=1, keepdims=True)

        def grad_probs(n, g_b):
            return dot(g_b, vs[: width(n), :], 1, 1)

        def grad_scores(weights, grad_p, dot_out):
            each = [w * (chunk(grad_p, j) - dot_out).astype(BF16) for j, w in enumerate(weights)]
            return jnp.concatenate(each, axis=1)

        def grads(n, grad_s, w_b, g_b):
            keys = width(n)
            store(1, n, dot(grad_s, ks[:keys, :], 1, 0) * SCALE)
            dks[:, :keys] += dot(load(0, n).T, grad_s, 1, 0)
            dvs[:, :keys] += dot(g_b.T, w_b, 1, 0)

        s, w, o, d, t = {}, {}, {}, {}, {}
        s[0] = scores(0)
        for n in range(nb + 1):
            if n < nb:
                w[n] = softmax(*s.pop(n))
            if n + 1 < nb:
                s[n + 1] = scores(n + 1)
            if n >= 1:
                t[n - 1] = grad_scores(w[n - 1][0], d.pop(n - 1), o[n - 1][1])
            if n < nb:
                o[n] = attend(n, w[n][2], w[n][1])
            if n >= 1:
                grads(n - 1, t.pop(n - 1), w.pop(n - 1)[2], o.pop(n - 1)[0])
            if n < nb:
                d[n] = grad_probs(n, o[n][0])
        for which in range(2):
            head_out(h, which).start()
        return carry

    lax.fori_loop(0, GROUP, one_head, 0)
    for s in range(SIDE):
        for at in range(SIDE):
            blank_copy(s, at).wait()
    dk = dks[:, :nr].T * SCALE
    dv = dvs[:, :nr].T
    for j, (second, first) in enumerate(places):
        terms[j, :, :HD] = dk[j * BLK : (j + 1) * BLK, :].astype(BF16)
        terms[j, :, HD:] = dv[j * BLK : (j + 1) * BLK, :].astype(BF16)
        for s, r in enumerate(term_refs):

            @pl.when((found[j] >= 0) & ((SIDE - second) % SIDE == s))
            def _():
                at = (SIDE - first) % SIDE
                pltpu.make_async_copy(terms.at[j], r.at[at], term_sem.at[j]).start()

    dk = dks[:, nr:].T * SCALE
    dv = dvs[:, nr:].T
    dfirst[:, :HD] = dk[:BLK, :]
    dfirst[:, HD:] = dv[:BLK, :]
    drest[:, :HD] = dk[BLK:, :].astype(BF16)
    drest[:, HD:] = dv[BLK:, :].astype(BF16)
    last = (
        pltpu.make_async_copy(dfirst, dfirst_ref, rest_sem.at[0]),
        pltpu.make_async_copy(drest, drest_ref, rest_sem.at[1]),
    )
    for c in last:
        c.start()
    for h in range(GROUP):
        for which in range(2):
            head_out(h, which).wait()
    for j in range(DMAX):

        @pl.when(found[j] >= 0)
        def _():
            pltpu.make_async_copy(terms.at[j], t0.at[0], term_sem.at[j]).wait()

    for c in last:
        c.wait()


def attention(here, parent, qg, kv, arrived, ends):
    span = qg.shape[0]
    nb = span // BLK
    keys = (DMAX + nb) * BLK

    anywhere = pl.BlockSpec(memory_space=pl.ANY)
    spec = pltpu.PrefetchScalarGridSpec(
        num_scalar_prefetch=2,
        grid=(),
        in_specs=[pl.BlockSpec(memory_space=pltpu.VMEM)] + [anywhere] * (2 + SIDE),
        out_specs=[anywhere] * (3 + SIDE),
        scratch_shapes=[
            pltpu.VMEM((keys, HD), BF16),
            pltpu.VMEM((keys, HD), BF16),
            pltpu.VMEM((HD, keys), F32),
            pltpu.VMEM((HD, keys), F32),
            pltpu.VMEM((nb, BLK, BLK), F32),
            pltpu.VMEM((GROUP, 2, span, HD), BF16),
            pltpu.VMEM((GROUP, 2, span, HD), BF16),
            pltpu.VMEM((DMAX, BLK, 2 * HD), BF16),
            pltpu.VMEM((BLK, 2 * HD), F32),
            pltpu.VMEM((span - BLK, 2 * HD), BF16),
            pltpu.VMEM((BLK, 2 * HD), BF16),
            pltpu.SemaphoreType.DMA((2,)),
            pltpu.SemaphoreType.DMA((GROUP, 2)),
            pltpu.SemaphoreType.DMA((DMAX, 2)),
            pltpu.SemaphoreType.DMA((GROUP, 2)),
            pltpu.SemaphoreType.DMA((SIDE * SIDE,)),
            pltpu.SemaphoreType.DMA((DMAX,)),
            pltpu.SemaphoreType.DMA((2,)),
        ],
    )
    pairs = GROUP * sum(DMAX + b + 1 for b in range(nb)) * BLK * BLK
    return pl.pallas_call(
        functools.partial(attention_kernel, nb),
        grid_spec=spec,
        out_shape=[
            jax.ShapeDtypeStruct(qg.shape, BF16),
            jax.ShapeDtypeStruct((BLK, 2 * HD), F32),
            jax.ShapeDtypeStruct((span - BLK, 2 * HD), BF16),
        ]
        + [jax.ShapeDtypeStruct((SIDE, BLK, 2 * HD), BF16)] * SIDE,
        compiler_params=pltpu.CompilerParams(vmem_limit_bytes=24 * 2**20),
        cost_estimate=pl.CostEstimate(
            flops=12 * pairs * HD, bytes_accessed=8 * span * 4 * HD, transcendentals=pairs
        ),
        name="tree_attention",
    )(here, parent, ends, qg, kv, *arrived)


def swap(x):
    return lax.all_to_all(x, "head", split_axis=0, concat_axis=0, tiled=True)


def local(queries, keys, values, grad_out, parent, subtree_end):
    n_head = lax.axis_size("head")
    here = jnp.stack([lax.axis_index("ctx"), lax.axis_index("head")]).astype(jnp.int32)
    rows = queries.shape[0]
    span = rows * n_head
    nb = span // BLK

    def by_head(x, y):
        both = [a.reshape(rows, n_head, -1) for a in (x, y)]
        return swap(jnp.concatenate(both, axis=2).transpose(1, 0, 2)).reshape(span, -1)

    kv = by_head(keys, values)
    first = kv[:BLK]
    by = {s: shifted(first, 1, s, True) for s in (2, 1, 3)}
    line = jnp.stack([first] + [by[s] for s in range(1, SIDE)])
    by = {s: shifted(line, 0, s, True) for s in (2, 1, 3)}
    arrived = [line] + [by[s] for s in range(1, SIDE)]
    qg = by_head(queries, grad_out)
    out, dfirst, drest, *terms = attention(here, parent, qg, kv, arrived, subtree_end.reshape(nb, BLK))

    def send_back(x):
        return swap(x.reshape(n_head, rows, -1))

    def by_token(x):
        return [a.reshape(rows, -1) for a in jnp.split(x.transpose(1, 0, 2), 2, axis=2)]

    out = send_back(out)

    by = {s: shifted(terms[s], 0, s, False) for s in (2, 1, 3)}
    got = [terms[0]] + [by[s] for s in range(1, SIDE)]
    own = lax.optimization_barrier(dfirst + sum(x[0].astype(F32) for x in got))
    for s in (2, 1, 3):
        part = sum(x[s].astype(F32) for x in got).astype(BF16)
        own = own + shifted(part, 1, s, False).astype(F32)
    dkv = jnp.concatenate([own.astype(BF16), drest], axis=0)
    out, dkv = lax.optimization_barrier((out, dkv))
    attn_out, grad_q = by_token(out)
    grad_k, grad_v = by_token(send_back(dkv))
    return attn_out, grad_q, grad_k, grad_v


def solution(mesh):
    placed = P(("ctx", "head"), None)
    return jax.shard_map(
        local,
        mesh=mesh,
        in_specs=(placed, placed, placed, placed, P(), P("ctx")),
        out_specs=(placed, placed, placed, placed),
        check_vma=False,
    )
```
